32 devices in a mesh: runs: 2 (over x), modes: 16 (over z, y, core).
Axes of the slice: x: 2, y: 2, z: 4, core: 2. Of those that a mesh axis runs over, the one named last changes fastest.
Arguments:
- amplitudes: float32 [8192, 2, 5, 512], P(('runs', 'modes')), parts along dimension 0, may hold values from -6 to 6
- mode_table: int32 [4096, 2], replicated, may hold values from 0 to 127, as said below
- slab_map: int32 [8], replicated, may hold values from 0 to 7, each once
- base_flow: float32 [1024], P('runs'), parts along dimension 0, may hold values from 0 to 1.5
- base_coupling: float32 [50, 512], P('runs'), parts along dimension 0, may hold values from -0.36 to 0.36
- slab_inverse: float32 [8, 64, 64], replicated
- wall_operator: float32 [64, 64], replicated, may hold values from -0.75 to 0.75
Outputs:
- marched: float32 [8192, 2, 5, 512], P(('runs', 'modes')), parts along dimension 0
The draws below stay inside these ranges and needn't reach their ends.
There are 2 independent parts, one for each index of `runs`. The reference program is written for one: setup_inputs(seed, part) draws one part's arguments, and reference() takes and returns one part's arrays. A program takes and returns all parts, laid end to end along the dimension named above; an argument that names none is the same for every part. Nothing has to cross between parts.
Inputs may be any that keep to these rules, and one draw needn't show every extreme that they name: `mode_table`: every cell of the 32 x 128 grid is named by exactly one mode; column 0 lies in 0 to 31. `slab_map`: each subdomain has its own slot.
All inputs are finite; a program needn't handle non-finite values.
Results may differ from the reference program's by a relative error of at most 0.0003.
Values sent between devices are 32-bit elements; how exact they have to be, the bound alone decides.
A program may use at most 192 MiB of HBM per device.

```python
import math
import jax
import jax.numpy as jnp
from jax import lax

M = 4096
NB = 128
NSUB = 8
P_SIZE = 64
SWEEPS = 3
STATIONS = 1
NW = 32
Y = 512


def draw_mode_table(key, part):
    order = jax.random.permutation(key, M).astype(jnp.int32)
    return jnp.stack([order // NB, order % NB], 1).astype(jnp.int32)


def draw_slab_inverse(key, part):
    first_key, second_key = jax.random.split(jax.random.fold_in(key, 7))
    diagonal = jax.random.uniform(first_key, (NSUB, P_SIZE), jnp.float32, 0.5, 0.9)
    spread = jax.random.normal(second_key, (NSUB, P_SIZE, P_SIZE), jnp.float32) * (0.15 / math.sqrt(P_SIZE))
    return spread + diagonal[:, :, None] * jnp.eye(P_SIZE, dtype=jnp.float32)[None]


def block_scale(key, dims, cuts, least, top_value):
    level = 1.0
    for dim, blocks in cuts:
        heights = jax.random.uniform(jax.random.fold_in(jax.random.fold_in(key, 6), dim), (blocks,), jnp.float32, least / len(cuts), top_value / len(cuts))
        level = level * jnp.repeat(jnp.exp(heights), dims[dim] // blocks).reshape((-1,) + (1,) * (len(dims) - 1 - dim))
    return level


def gaussian(stream_key, shape, deviation, reach, shards=(), kind=jnp.bfloat16):
    drawn = deviation * jax.random.normal(stream_key, shape, jnp.float32)
    if shards:
        drawn = drawn * block_scale(stream_key, shape, shards, -0.22, 0.18)
    return jnp.clip(drawn, -reach, reach).astype(kind)


def setup_inputs(seed: int = 0, part: int = 0) -> dict:
    key_list = jax.random.split(jax.random.key(seed), 8)
    own_keys = jax.random.split(jax.random.fold_in(key_list[7], part), 8)
    return {
        "amplitudes": gaussian(own_keys[0], (M, 2, 5, Y), 1.0, 6.0, ((0, 16),), jnp.float32),
        "mode_table": draw_mode_table(jax.random.fold_in(key_list[7], 71), part),
        "slab_map": jax.random.permutation(key_list[2], NSUB).astype(jnp.int32),
        "base_flow": jnp.clip(jax.random.uniform(own_keys[3], (Y,), jnp.float32, 0.0, 1.5), 0.0, 1.5),
        "base_coupling": gaussian(own_keys[4], (25, Y), 0.06, 0.36, (), jnp.float32),
        "slab_inverse": draw_slab_inverse(jax.random.fold_in(key_list[7], 71), part),
        "wall_operator": gaussian(key_list[6], (P_SIZE, P_SIZE), P_SIZE ** -0.5, 0.75, (), jnp.float32),
    }


precise = lax.Precision.HIGHEST
omega_step = 0.01
phase_gain = 0.2
march_step = 0.2
coupling = 0.3

def twiddle(length):
    counter = jnp.arange(length, dtype=jnp.int32)
    product = counter[:, None] * counter[None, :] % length
    angles = product.astype(jnp.float32) * (2.0 * math.pi / length)
    return (jnp.cos(angles), jnp.sin(angles))

def mode_tables(mode_table):
    omega_index = mode_table[:, 0]
    beta_index = mode_table[:, 1]
    signed = jnp.where(beta_index >= NB // 2, beta_index - NB, beta_index)
    wavenum = 2.0 * signed.astype(jnp.float32) / NB
    frequency = omega_step * omega_index.astype(jnp.float32)
    grid_pos = (omega_index * NB + beta_index).astype(jnp.int32)
    mode_at = jnp.zeros((M,), jnp.int32).at[grid_pos].set(jnp.arange(M, dtype=jnp.int32))
    return (wavenum, frequency, grid_pos, mode_at)

def synthesize(real_part, imag_part, tables, factor):
    cos_omega, sin_omega, cos_beta, sin_beta = tables
    mixed_re = jnp.einsum('...wb,bz->...wz', real_part, cos_beta, precision=precise) - jnp.einsum('...wb,bz->...wz', imag_part, sin_beta, precision=precise)
    mixed_im = jnp.einsum('...wb,bz->...wz', real_part, sin_beta, precision=precise) + jnp.einsum('...wb,bz->...wz', imag_part, cos_beta, precision=precise)
    physical = jnp.einsum('...wz,wt->...tz', mixed_re, cos_omega, precision=precise) - jnp.einsum('...wz,wt->...tz', mixed_im, sin_omega, precision=precise)
    return physical * factor

def analyze(physical, tables, factor):
    cos_omega, sin_omega, cos_beta, sin_beta = tables
    half_re = jnp.einsum('...tz,zb->...tb', physical, cos_beta, precision=precise)
    half_im = -jnp.einsum('...tz,zb->...tb', physical, sin_beta, precision=precise)
    coef_re = jnp.einsum('...tb,tw->...wb', half_re, cos_omega, precision=precise) + jnp.einsum('...tb,tw->...wb', half_im, sin_omega, precision=precise)
    coef_im = jnp.einsum('...tb,tw->...wb', half_im, cos_omega, precision=precise) - jnp.einsum('...tb,tw->...wb', half_re, sin_omega, precision=precise)
    return (coef_re * factor, coef_im * factor)

def forcing(normal_vel, spanwise_vel, wall_grad, span_grad, tables, factor):
    vel_v = synthesize(normal_vel[0], normal_vel[1], tables, factor)
    vel_w = synthesize(spanwise_vel[0], spanwise_vel[1], tables, factor)
    grad_y = synthesize(wall_grad[0], wall_grad[1], tables, factor)
    grad_z = synthesize(span_grad[0], span_grad[1], tables, factor)
    product = -(vel_v[None] * grad_y + vel_w[None] * grad_z)
    return analyze(product, tables, factor)

def wall_derivative(values, wall_operator):
    slab_width = wall_operator.shape[0]
    slab_count = values.shape[3] // slab_width
    blocks = values.reshape(values.shape[:3] + (slab_count, slab_width))
    return jnp.einsum('ij,abcsj->abcsi', wall_operator, blocks, precision=precise).reshape(values.shape)

def interface(iterate, slab_map, slab_count, slab_width):
    blocks = iterate.reshape(iterate.shape[:3] + (slab_count, slab_width))
    ordered = jnp.take(blocks, slab_map, axis=3)
    edge_zero = jnp.zeros(blocks.shape[:3] + (1,), jnp.float32)
    lower_rim = jnp.concatenate([edge_zero, ordered[..., :-1, slab_width - 1]], 3)
    upper_rim = jnp.concatenate([ordered[..., 1:, 0], edge_zero], 3)
    middle = jnp.zeros(blocks.shape[:4] + (slab_width - 2,), jnp.float32)
    joined = jnp.concatenate([lower_rim[..., None], middle, upper_rim[..., None]], 4)
    inverse = jnp.zeros((slab_count,), jnp.int32).at[slab_map].set(jnp.arange(slab_count, dtype=jnp.int32))
    return jnp.take(joined, inverse, axis=3).reshape(iterate.shape)

def relaxation(iterate, right_side, wave_local, freq_local, crossflow, base_coupling, slab_inverse, slab_map):
    points = iterate.shape[3]
    slab_count = slab_inverse.shape[0]
    slab_width = slab_inverse.shape[1]
    matrix = base_coupling.reshape(5, 5, points)
    coupled = jnp.einsum('kjy,acjy->acky', matrix, iterate, precision=precise)
    rotation = phase_gain * wave_local[:, None] * crossflow[None, :] - freq_local[:, None]
    applied = jnp.stack([coupled[:, 0] - rotation[:, None, :] * iterate[:, 1], coupled[:, 1] + rotation[:, None, :] * iterate[:, 0]], 1)
    residual_in = right_side - applied + coupling * interface(iterate, slab_map, slab_count, slab_width)
    blocks = residual_in.reshape(iterate.shape[:3] + (slab_count, slab_width))
    return jnp.einsum('sij,acvsj->acvsi', slab_inverse, blocks, precision=precise).reshape(iterate.shape)

def reference(amplitudes, mode_table, slab_map, base_flow, base_coupling, slab_inverse, wall_operator):
    wavenum, frequency, grid_pos, mode_at = mode_tables(mode_table)
    tables = twiddle(NW) + twiddle(NB)
    factor = 1.0 / math.sqrt(M)
    current = amplitudes
    for station in range(STATIONS):
        gradient = wall_derivative(current, wall_operator)
        span = jnp.stack([-wavenum[:, None, None] * current[:, 1], wavenum[:, None, None] * current[:, 0]], 1)
        fields = jnp.concatenate([current[:, :, 2:4], gradient, span], 2)

        def block_forcing(block_index):
            piece = lax.dynamic_slice_in_dim(fields, (block_index * P_SIZE).astype(jnp.int32), P_SIZE, 3)
            gridded = jnp.transpose(piece, (1, 2, 3, 0))[..., mode_at].reshape(2, 12, P_SIZE, NW, NB)
            coef_re, coef_im = forcing(gridded[:, 0], gridded[:, 1], gridded[:, 2:7], gridded[:, 7:12], tables, factor)
            return jnp.stack([coef_re, coef_im], 0).reshape(2, 5, P_SIZE, M)[..., grid_pos]
        pieces = lax.map(block_forcing, jnp.arange(NSUB, dtype=jnp.int32))
        nonlinear = jnp.transpose(pieces, (4, 1, 2, 0, 3)).reshape(M, 2, 5, NSUB * P_SIZE)
        crossflow = base_flow + current[mode_at[0], 0, 3]
        right_side = current + march_step * nonlinear
        iterate = current
        for sweep_index in range(SWEEPS):
            iterate = relaxation(iterate, right_side, wavenum, frequency, crossflow, base_coupling, slab_inverse, slab_map)
        current = iterate
    return current
```

```python
import math

import jax
import jax.numpy as jnp
import ml_dtypes
import numpy as np
from jax import lax
from jax.experimental import pallas as pl
from jax.experimental.pallas import tpu as pltpu
from jax.sharding import PartitionSpec as P

M = 4096
NB = 128
SWEEPS = 3
NW = 32


precise = lax.Precision.HIGHEST
omega_step = 0.01
phase_gain = 0.2
march_step = 0.2
coupling = 0.3


def twiddle(length):
    counter = jnp.arange(length, dtype=jnp.int32)
    product = counter[:, None] * counter[None, :] % length
    angles = product.astype(jnp.float32) * (2.0 * math.pi / length)
    return (jnp.cos(angles), jnp.sin(angles))


def mode_tables(mode_table):
    omega_index = mode_table[:, 0]
    beta_index = mode_table[:, 1]
    signed = jnp.where(beta_index >= NB // 2, beta_index - NB, beta_index)
    wavenum = 2.0 * signed.astype(jnp.float32) / NB
    frequency = omega_step * omega_index.astype(jnp.float32)
    grid_pos = omega_index * NB + beta_index
    mode_at = jnp.zeros((M,), jnp.int32).at[grid_pos].set(jnp.arange(M, dtype=jnp.int32))
    return (wavenum, frequency, grid_pos, mode_at)


def synthesize(real_part, imag_part, tables, factor):
    cos_omega, sin_omega, cos_beta, sin_beta = tables
    mixed_re = jnp.einsum("...wb,bz->...wz", real_part, cos_beta, precision=precise) - jnp.einsum(
        "...wb,bz->...wz", imag_part, sin_beta, precision=precise
    )
    mixed_im = jnp.einsum("...wb,bz->...wz", real_part, sin_beta, precision=precise) + jnp.einsum(
        "...wb,bz->...wz", imag_part, cos_beta, precision=precise
    )
    physical = jnp.einsum("...wz,wt->...tz", mixed_re, cos_omega, precision=precise) - jnp.einsum(
        "...wz,wt->...tz", mixed_im, sin_omega, precision=precise
    )
    return physical * factor


def analyze(physical, tables, factor):
    cos_omega, sin_omega, cos_beta, sin_beta = tables
    half_re = jnp.einsum("...tz,zb->...tb", physical, cos_beta, precision=precise)
    half_im = -jnp.einsum("...tz,zb->...tb", physical, sin_beta, precision=precise)
    coef_re = jnp.einsum("...tb,tw->...wb", half_re, cos_omega, precision=precise) + jnp.einsum(
        "...tb,tw->...wb", half_im, sin_omega, precision=precise
    )
    coef_im = jnp.einsum("...tb,tw->...wb", half_im, cos_omega, precision=precise) - jnp.einsum(
        "...tb,tw->...wb", half_re, sin_omega, precision=precise
    )
    return (coef_re * factor, coef_im * factor)


def forcing(normal_vel, spanwise_vel, wall_grad, span_grad, tables, factor):
    vel_v = synthesize(normal_vel[0], normal_vel[1], tables, factor)
    vel_w = synthesize(spanwise_vel[0], spanwise_vel[1], tables, factor)
    grad_y = synthesize(wall_grad[0], wall_grad[1], tables, factor)
    grad_z = synthesize(span_grad[0], span_grad[1], tables, factor)
    product = -(vel_v[None] * grad_y + vel_w[None] * grad_z)
    return analyze(product, tables, factor)


def wall_derivative(values, wall_operator):
    slab_width = wall_operator.shape[0]
    slab_count = values.shape[3] // slab_width
    blocks = values.reshape(values.shape[:3] + (slab_count, slab_width))
    return jnp.einsum("ij,abcsj->abcsi", wall_operator, blocks, precision=precise).reshape(
        values.shape
    )


def interface_table(slab_map, slab_count, slab_width):
    inverse = (
        jnp.zeros((slab_count,), jnp.int32)
        .at[slab_map]
        .set(jnp.arange(slab_count, dtype=jnp.int32))
    )
    position = jnp.arange(slab_count * slab_width, dtype=jnp.int32)
    slot_of = position // slab_width
    within = position % slab_width
    domain = inverse[slot_of]
    below = slab_map[jnp.maximum(domain - 1, 0)] * slab_width + (slab_width - 1)
    above = slab_map[jnp.minimum(domain + 1, slab_count - 1)] * slab_width
    lower_ok = (within == 0) & (domain > 0)
    upper_ok = (within == slab_width - 1) & (domain < slab_count - 1)
    source = jnp.where(lower_ok, below, jnp.where(upper_ok, above, 0))
    weight = (lower_ok | upper_ok).astype(jnp.float32)
    return (source, weight)


def relaxation(iterate, right_side, rotation, matrix, slab_inverse, source, weight):
    slab_count = slab_inverse.shape[0]
    slab_width = slab_inverse.shape[1]
    coupled = jnp.einsum("kjy,acjy->acky", matrix, iterate, precision=precise)
    applied = jnp.stack(
        [
            coupled[:, 0] - rotation[:, None, :] * iterate[:, 1],
            coupled[:, 1] + rotation[:, None, :] * iterate[:, 0],
        ],
        1,
    )
    rims = jnp.take(iterate, source, axis=3) * weight
    residual_in = right_side - applied + coupling * rims
    blocks = residual_in.reshape(iterate.shape[:3] + (slab_count, slab_width))
    return jnp.einsum("sij,acvsj->acvsi", slab_inverse, blocks, precision=precise).reshape(
        iterate.shape
    )


def local(amplitudes, mode_table, slab_map, base_flow, base_coupling, slab_inverse, wall_operator):
    local_modes = amplitudes.shape[0]
    wall_points = amplitudes.shape[3]
    groups = lax.axis_size("modes")
    point_share = wall_points // groups
    wavenum, frequency, grid_pos, mode_at = mode_tables(mode_table)
    first_mode = lax.axis_index("modes") * local_modes
    wave_local = lax.dynamic_slice_in_dim(wavenum, first_mode, local_modes)
    freq_local = lax.dynamic_slice_in_dim(frequency, first_mode, local_modes)
    tables = twiddle(NW) + twiddle(NB)
    factor = 1.0 / math.sqrt(M)
    source, weight = interface_table(slab_map, slab_inverse.shape[0], slab_inverse.shape[1])
    matrix = base_coupling.reshape(5, 5, wall_points)
    gradient = wall_derivative(amplitudes, wall_operator)
    span = jnp.stack(
        [
            -wave_local[:, None, None] * amplitudes[:, 1],
            wave_local[:, None, None] * amplitudes[:, 0],
        ],
        1,
    )
    fields = jnp.concatenate([amplitudes[:, :, 2:4], gradient, span], 2)
    field_count = fields.shape[2]
    channels = 2 * field_count
    outgoing = jnp.transpose(
        fields.reshape(local_modes, channels, groups, point_share), (1, 2, 3, 0)
    ).reshape(channels, groups, point_share * local_modes)
    incoming = lax.all_to_all(outgoing, "modes", split_axis=1, concat_axis=1, tiled=True)
    by_mode = jnp.transpose(
        incoming.reshape(channels, groups, point_share, local_modes), (0, 2, 1, 3)
    ).reshape(channels, point_share, M)
    gridded = by_mode[..., mode_at].reshape(2, field_count, point_share, NW, NB)
    normal_vel = gridded[:, 0]
    spanwise_vel = gridded[:, 1]
    wall_grad = gridded[:, 2:7]
    span_grad = gridded[:, 7:12]
    mean_crossflow = lax.all_gather(spanwise_vel[0, :, 0, 0], "modes", axis=0, tiled=True)
    coef_re, coef_im = forcing(normal_vel, spanwise_vel, wall_grad, span_grad, tables, factor)
    packed = jnp.stack([coef_re, coef_im], 0).reshape(10, point_share, M)[..., grid_pos]
    sendback = jnp.transpose(
        packed.reshape(10, point_share, groups, local_modes), (0, 2, 1, 3)
    ).reshape(10, groups, point_share * local_modes)
    returned = lax.all_to_all(sendback, "modes", split_axis=1, concat_axis=1, tiled=True)
    nonlinear = jnp.transpose(
        returned.reshape(10, groups, point_share, local_modes), (3, 0, 1, 2)
    ).reshape(local_modes, 2, 5, wall_points)
    crossflow = base_flow + mean_crossflow
    rotation = phase_gain * wave_local[:, None] * crossflow[None, :] - freq_local[:, None]
    right_side = amplitudes + march_step * nonlinear
    iterate = amplitudes
    for sweep_index in range(SWEEPS):
        iterate = relaxation(iterate, right_side, rotation, matrix, slab_inverse, source, weight)
    return iterate


F32 = jnp.float32
BF16 = jnp.bfloat16
VMEM_BYTES = 56 * 1024 * 1024
SHARE = 32
LANES = 128


def split_np(values):
    high = values.astype(np.float32).astype(ml_dtypes.bfloat16)
    low = (values - high.astype(np.float64)).astype(np.float32).astype(ml_dtypes.bfloat16)
    return high, low


def split(values):
    high = values.astype(BF16)
    low = (values - high.astype(F32)).astype(BF16)
    return high, low


def dot(left, right):
    return jnp.dot(left, right, preferred_element_type=F32)


def dot3(left, right):
    return dot(left[0], right[0]) + (dot(left[0], right[1]) + dot(left[1], right[0]))


def synthesis_matrix():
    index = np.arange(NB)
    angle = 2.0 * np.pi * (index[:, None] * index[None, :] % NB) / NB
    cos, sin = np.cos(angle), np.sin(angle)
    signed = np.where(index >= NB // 2, index - NB, index)
    wave = (2.0 * signed / NB)[None, :]
    rows = [
        np.concatenate([cos, -sin], 1),
        np.concatenate([sin, cos], 1),
        np.concatenate([-sin * wave, -cos * wave], 1),
        np.concatenate([cos * wave, -sin * wave], 1),
    ]
    return np.concatenate(rows, 0) / math.sqrt(M)


def analysis_matrix():
    index = np.arange(NB)
    angle = 2.0 * np.pi * (index[:, None] * index[None, :] % NB) / NB
    cos, sin = np.cos(angle), np.sin(angle)
    rows = [np.concatenate([cos, sin], 1), np.concatenate([-sin, cos], 1)]
    return np.concatenate(rows, 0) / math.sqrt(M)


def weighted(terms, weights):
    total = None
    for term, weight in zip(terms, weights):
        if abs(weight) < 1e-12:
            continue
        if abs(weight - 1.0) < 1e-12:
            part = term
        elif abs(weight + 1.0) < 1e-12:
            part = -term
        else:
            part = term * np.float32(weight)
        total = part if total is None else total + part
    return total


def cosine_sums(terms):
    half, quarter = NW // 2, NW // 4
    out = [None] * (half + 1)
    for t in range(quarter + 1):
        even = weighted(terms[0::2], [math.cos(2 * math.pi * w * t / NW) for w in range(0, half + 1, 2)])
        odd = weighted(terms[1::2], [math.cos(2 * math.pi * w * t / NW) for w in range(1, half + 1, 2)])
        if odd is None:
            out[t] = even
            out[half - t] = even
        else:
            out[t] = even + odd
            out[half - t] = even - odd
    return out


def sine_sums(terms):
    half, quarter = NW // 2, NW // 4
    out = [None] * half
    for t in range(1, quarter + 1):
        even = weighted(terms[2::2], [math.sin(2 * math.pi * w * t / NW) for w in range(2, half, 2)])
        odd = weighted(terms[1::2], [math.sin(2 * math.pi * w * t / NW) for w in range(1, half, 2)])
        if even is None:
            out[t] = odd
        else:
            out[t] = odd + even
            out[half - t] = odd - even
    return out


def lane_group(shape):
    return lax.broadcasted_iota(jnp.int32, shape, len(shape) - 1) // SHARE


def shifted(values, groups):
    groups = groups % 4
    return values if groups == 0 else pltpu.roll(values, groups * SHARE, values.ndim - 1)


def join(pieces, which):
    low = jnp.where(which == 0, pieces[0], pieces[1])
    high = jnp.where(which == 2, pieces[2], pieces[3])
    return jnp.where(which < 2, low, high)


def pack_kernel(amp_ref, out_ref):
    half = amp_ref.shape[1] // 2
    full = 2 * half
    which = lane_group((8, LANES))

    def body(step, carry):
        row = pl.multiple_of(step * 8, 8)
        for tile in range(4):
            lanes = pl.ds(tile * LANES, LANES)
            rims = []
            for side in range(2):
                rows = pl.ds(row + side * half, 8)
                parts = [amp_ref[c, rows, lanes] for c in range(10)]
                rims += [parts[4], parts[9]]
                for q in range(4):
                    dest = tile * 4 + q
                    for block, first in ((0, 0), (1, 5)):
                        out_ref[dest, pl.ds(row + side * half + block * full, 8), :] = join(
                            [shifted(parts[first + k], k - q) for k in range(4)], which
                        )
            for q in range(4):
                out_ref[tile * 4 + q, pl.ds(row + 2 * full, 8), :] = join(
                    [shifted(rims[k], k - q) for k in range(4)], which
                )
        return carry

    lax.fori_loop(0, half // 8, body, 0)


def physical_kernel(pos_ref, in_ref, high_ref, low_ref, field_ref, span_ref, mean_ref, ga, gb, gc, mid):
    sources = in_ref.shape[0]
    half = M // sources // 2
    full = 2 * half

    def spread(source, carry):
        def rows_of(step, inner):
            row = pl.multiple_of(step * 8, 8)
            rest = in_ref[source, pl.ds(row + 2 * full, 8), :]
            for side in range(2):
                first = row + side * half
                a8 = in_ref[source, pl.ds(first, 8), :]
                b8 = in_ref[source, pl.ds(first + full, 8), :]
                c8 = shifted(rest, 2 * side)
                for u in range(8):
                    where = pos_ref[source * full + first + u]
                    ga[pl.ds(where, 1), :] = a8[u : u + 1, :]
                    gb[pl.ds(where, 1), :] = b8[u : u + 1, :]
                    gc[pl.ds(where, 1), :] = c8[u : u + 1, :]
            return inner

        return lax.fori_loop(0, half // 8, rows_of, carry)

    lax.fori_loop(0, sources, spread, 0)
    mean_ref[...] = jnp.broadcast_to(ga[0:1, :], mean_ref.shape)

    first_group = lane_group((NB, LANES)) == 0

    def beta_sum(omega, carry):
        rows = pl.ds(pl.multiple_of(omega * NB, NB), NB)
        rest = gc[rows, :]
        data = jnp.concatenate(
            [
                jnp.concatenate([ga[rows, :], rest], 1),
                jnp.concatenate([gb[rows, :], shifted(rest, 3)], 1),
            ],
            0,
        )
        out = dot3((high_ref[...], low_ref[...]), split(data))
        mid[omega, 0 : 4 * NB, :] = out[:, :LANES]
        tail = out[:, LANES:]
        for part in range(2):
            mid[omega, (4 + part) * NB : (5 + part) * NB, :] = jnp.where(
                first_group,
                tail[part * NB : (part + 1) * NB],
                shifted(tail[(2 + part) * NB : (3 + part) * NB], 1),
            )
        return carry

    lax.fori_loop(0, NW, beta_sum, 0)

    which = lane_group((8, LANES))

    def omega_sum(step, carry):
        row = pl.multiple_of(step * 8, 8)
        for group in range(3):
            re = [mid[w, pl.ds(row + 2 * group * NB, 8), :] for w in range(NW)]
            im = [mid[w, pl.ds(row + (2 * group + 1) * NB, 8), :] for w in range(NW)]
            half_w = NW // 2
            cos_terms = [re[0]] + [re[w] + re[NW - w] for w in range(1, half_w)] + [re[half_w]]
            sin_terms = [None] + [im[w] - im[NW - w] for w in range(1, half_w)]
            even = cosine_sums(cos_terms)
            odd = sine_sums(sin_terms)
            out = [None] * NW
            out[0] = even[0]
            out[half_w] = even[half_w]
            for t in range(1, half_w):
                out[t] = even[t] - odd[t]
                out[NW - t] = even[t] + odd[t]
            if group < 2:
                target = (field_ref, span_ref)[group]
                for t in range(NW):
                    target[t, pl.ds(row, 8), :] = out[t]
            else:
                for t in range(8):
                    for target, start in ((field_ref, 0), (span_ref, 1)):
                        target[NW + t, pl.ds(row, 8), :] = join(
                            [shifted(out[t + 8 * k], k - start) for k in range(4)], which
                        )
        return carry

    lax.fori_loop(0, NB // 8, omega_sum, 0)


def force_kernel(
    pos_ref, field_ref, other_ref, span_ref, mean_ref, wall_ref, high_ref, low_ref, out_ref,
    force, mid, na, nb, nc, rest_rows,
):
    sources = out_ref.shape[0]
    half = M // sources // 2
    full = 2 * half
    wall = split(wall_ref[...])

    def products(step, carry):
        which = lane_group((NB, LANES))

        def gradient(row):
            both = jnp.concatenate([field_ref[row], other_ref[row]], 1)
            return dot3(split(both), wall)

        packed_v = packed_w = None
        for k in range(4):
            t = step + 8 * k
            own = field_ref[t]
            v = join([shifted(own, j - 2) for j in range(4)], which)
            w = join([shifted(own, j - 3) for j in range(4)], which)
            force[t] = -(v * gradient(t) + w * span_ref[t])
            packed_v = v if k == 0 else jnp.where(which == k, v, packed_v)
            packed_w = w if k == 0 else jnp.where(which == k, w, packed_w)
        t = step + NW
        force[t] = -(packed_v * gradient(t) + packed_w * span_ref[t])
        return carry

    lax.fori_loop(0, 8, products, 0)

    half_w = NW // 2

    def time_sum(step, carry):
        row = pl.multiple_of(step * 8, 8)
        rows = pl.ds(row, 8)
        for group in range(2):
            if group == 0:
                values = [force[t, rows, :] for t in range(NW)]
            else:
                packed = [force[NW + t, rows, :] for t in range(8)]
                values = [shifted(packed[t % 8], -(t // 8)) for t in range(NW)]
            cos_terms = (
                [values[0]]
                + [values[t] + values[NW - t] for t in range(1, half_w)]
                + [values[half_w]]
            )
            sin_terms = [None] + [values[NW - t] - values[t] for t in range(1, half_w)]
            even = cosine_sums(cos_terms)
            odd = sine_sums(sin_terms)
            lanes = slice(group * LANES, (group + 1) * LANES)
            zero = jnp.zeros((8, LANES), F32)
            for w in range(half_w + 1):
                mid[w, rows, lanes] = even[w]
                mid[w, pl.ds(row + NB, 8), lanes] = odd[w] if 0 < w < half_w else zero
        return carry

    lax.fori_loop(0, NB // 8, time_sum, 0)

    first_group = lane_group((NB, LANES)) == 0

    def span_sum(omega, carry):
        out = dot3((high_ref[...], low_ref[...]), split(mid[omega]))
        rows = pl.ds(pl.multiple_of(omega * NB, NB), NB)
        na[rows, :] = out[:NB, :LANES]
        nb[rows, :] = out[NB:, :LANES]
        nc[rows, :] = jnp.where(first_group, out[:NB, LANES:], shifted(out[NB:, LANES:], 1))
        return carry

    lax.fori_loop(0, half_w + 1, span_sum, 0)

    which = lane_group((8, LANES))

    def collect(source, carry):
        def rows_of(step, inner):
            row = pl.multiple_of(step * 8, 8)
            for side in range(2):
                first = row + side * half
                for u in range(8):
                    where = pos_ref[source * full + first + u]
                    out_ref[source, pl.ds(first + u, 1), :] = na[pl.ds(where, 1), :]
                    out_ref[source, pl.ds(first + full + u, 1), :] = nb[pl.ds(where, 1), :]
                    rest_rows[side, pl.ds(row + u, 1), :] = nc[pl.ds(where, 1), :]
            return inner

        lax.fori_loop(0, half // 8, rows_of, 0)
        wide = lane_group((half, LANES)) < 2
        out_ref[source, 2 * full : 2 * full + half, :] = jnp.where(
            wide, rest_rows[0], shifted(rest_rows[1], 2)
        )
        out_ref[source, 2 * full + half : 2 * full + half + 8, :] = mean_ref[...]
        return carry

    lax.fori_loop(0, sources, collect, 0)


def sweep_kernel(
    amp_ref, back_ref, base_ref, matrix_ref, inverse_ref, rim_ref, wave_ref, freq_ref, sign_ref,
    out_ref, right, current, residual, flow,
):
    half = amp_ref.shape[1] // 2
    full = 2 * half
    rows_in = 16
    which = lane_group((rows_in, LANES))
    which8 = lane_group((8, LANES))
    for tile in range(4):
        mean = join(
            [shifted(back_ref[4 * tile + k, 2 * full + half : 2 * full + half + 8, :], k - 3) for k in range(4)],
            which8,
        )
        flow[:, tile * LANES : (tile + 1) * LANES] = mean + base_ref[:, tile * LANES : (tile + 1) * LANES]
    inverse = [split(inverse_ref[g]) for g in range(2)]

    def chunk(step, carry):
        row = pl.multiple_of(step * rows_in, rows_in)
        for tile in range(4):
            lanes = slice(tile * LANES, (tile + 1) * LANES)
            rest = [back_ref[4 * tile + k, pl.ds(row + 2 * full, rows_in), :] for k in range(4)]
            for side in range(2):
                rows = pl.ds(row + side * half, rows_in)
                sign = sign_ref[rows, :]
                for part in range(2):
                    got = [
                        back_ref[4 * tile + k, pl.ds(row + side * half + part * full, rows_in), :]
                        for k in range(4)
                    ]
                    for c in range(5):
                        if c < 4:
                            value = join([shifted(got[k], k - c) for k in range(4)], which)
                        else:
                            value = join([shifted(rest[k], k - 2 * side - part) for k in range(4)], which)
                        if part == 1:
                            value = value * sign
                        own = amp_ref[5 * part + c, rows, lanes]
                        place = slice((5 * part + c) * 32 + side * 16, (5 * part + c) * 32 + side * 16 + 16)
                        current[place, lanes] = own
                        right[place, lanes] = own + march_step * value

        for sweep in range(SWEEPS):
            high, low = split(current[...])
            residual[...] = right[...] + coupling * (dot(high, rim_ref[...]) + dot(low, rim_ref[...]))
            for tile in range(4):
                lanes = slice(tile * LANES, (tile + 1) * LANES)
                for side in range(2):
                    rows = pl.ds(row + side * half, rows_in)
                    rotation = phase_gain * wave_ref[rows, :] * flow[0:1, lanes] - freq_ref[rows, :]
                    x = [current[c * 32 + side * 16 : c * 32 + side * 16 + 16, lanes] for c in range(10)]
                    for part in range(2):
                        for c in range(5):
                            total = rotation * x[5 * (1 - part) + c]
                            if part == 0:
                                total = -total
                            for j in range(5):
                                total = total + matrix_ref[5 * c + j : 5 * c + j + 1, lanes] * x[5 * part + j]
                            place = slice((5 * part + c) * 32 + side * 16, (5 * part + c) * 32 + side * 16 + 16)
                            residual[place, lanes] = residual[place, lanes] - total
            for g in range(2):
                lanes = slice(g * 256, (g + 1) * 256)
                current[:, lanes] = dot3(split(residual[:, lanes]), inverse[g])
        for c in range(10):
            for side in range(2):
                out_ref[c, pl.ds(row + side * half, rows_in), :] = current[
                    c * 32 + side * 16 : c * 32 + side * 16 + 16, :
                ]
        return carry

    lax.fori_loop(0, half // rows_in, chunk, 0)


def local_fast(amplitudes, mode_table, slab_map, base_flow, base_coupling, slab_inverse, wall_operator):
    local_modes = amplitudes.shape[0]
    points = amplitudes.shape[3]
    groups = lax.axis_size("modes")
    me = lax.axis_index("modes")
    half = local_modes // 2
    vmem = pl.BlockSpec(memory_space=pltpu.VMEM)
    smem = pl.BlockSpec(memory_space=pltpu.SMEM)
    params = pltpu.CompilerParams(vmem_limit_bytes=VMEM_BYTES)
    width = slab_inverse.shape[1]

    omega_index = mode_table[:, 0]
    beta_index = mode_table[:, 1]
    grid_pos = omega_index * NB + beta_index
    mirrored = omega_index > NW // 2
    back_pos = jnp.where(mirrored, (NW - omega_index) * NB + (NB - beta_index) % NB, grid_pos)
    local_table = lax.dynamic_slice_in_dim(mode_table, me * local_modes, local_modes)
    omega_local = local_table[:, 0:1]
    beta_local = local_table[:, 1:2]
    signed = jnp.where(beta_local >= NB // 2, beta_local - NB, beta_local)
    wave_local = 2.0 * signed.astype(F32) / NB
    freq_local = omega_step * omega_local.astype(F32)
    sign_local = jnp.where(omega_local > NW // 2, -1.0, 1.0).astype(F32)

    part = lax.rem(me, 2) * SHARE
    rows = lax.dynamic_slice_in_dim(wall_operator, part, SHARE, 0)
    mine = lax.dynamic_slice_in_dim(rows, part, SHARE, 1)
    theirs = lax.dynamic_slice_in_dim(rows, SHARE - part, SHARE, 1)
    eye = jnp.eye(4, dtype=F32)

    def blocks(value):
        size = value.shape[0]
        return (eye[:, None, :, None] * value.T[None, :, None, :]).reshape(4 * size, 4 * size)

    wall = jnp.concatenate([blocks(mine), blocks(theirs)], 0)
    turned = jnp.swapaxes(slab_inverse, 1, 2).reshape(2, 4, width, 1, width)
    inverse = (turned * eye[None, :, None, :, None]).reshape(2, 4 * width, 4 * width)
    source, weight = interface_table(slab_map, slab_inverse.shape[0], width)
    rim = ((jnp.arange(points, dtype=jnp.int32)[:, None] == source[None, :]) & (weight[None, :] > 0)).astype(BF16)

    amp = jnp.transpose(amplitudes, (1, 2, 0, 3)).reshape(10, local_modes, points)
    message = pl.pallas_call(
        pack_kernel,
        out_shape=jax.ShapeDtypeStruct((groups, 5 * half, LANES), F32),
        in_specs=[vmem],
        out_specs=vmem,
        compiler_params=params,
        name="pack",
    )(amp)
    arrived = lax.all_to_all(message, "modes", split_axis=0, concat_axis=0, tiled=True)

    high, low = split_np(synthesis_matrix())
    block = jax.ShapeDtypeStruct((NW + 8, NB, LANES), F32)
    field, span, mean = pl.pallas_call(
        physical_kernel,
        out_shape=[block, block, jax.ShapeDtypeStruct((8, LANES), F32)],
        in_specs=[smem, vmem, vmem, vmem],
        out_specs=[vmem, vmem, vmem],
        scratch_shapes=[pltpu.VMEM((M, LANES), F32)] * 3 + [pltpu.VMEM((NW, 6 * NB, LANES), F32)],
        compiler_params=params,
        name="physical",
    )(grid_pos, arrived, jnp.asarray(high), jnp.asarray(low))
    other = lax.ppermute(field, "modes", [(i, i ^ 1) for i in range(groups)])

    high, low = split_np(analysis_matrix())
    rows_back = (NW // 2 + 1) * NB
    sendback = pl.pallas_call(
        force_kernel,
        out_shape=jax.ShapeDtypeStruct((groups, 5 * half + 8, LANES), F32),
        in_specs=[smem] + [vmem] * 7,
        out_specs=vmem,
        scratch_shapes=[
            pltpu.VMEM((NW + 8, NB, LANES), F32),
            pltpu.VMEM((NW // 2 + 1, 2 * NB, 2 * LANES), F32),
        ]
        + [pltpu.VMEM((rows_back, LANES), F32)] * 3
        + [pltpu.VMEM((2, half, LANES), F32)],
        compiler_params=params,
        name="force",
    )(back_pos, field, other, span, mean, wall, jnp.asarray(high), jnp.asarray(low))
    returned = lax.all_to_all(sendback, "modes", split_axis=0, concat_axis=0, tiled=True)

    marched = pl.pallas_call(
        sweep_kernel,
        out_shape=jax.ShapeDtypeStruct((10, local_modes, points), F32),
        in_specs=[vmem] * 9,
        out_specs=vmem,
        scratch_shapes=[pltpu.VMEM((320, points), F32)] * 3 + [pltpu.VMEM((8, points), F32)],
        compiler_params=params,
        name="sweeps",
    )(amp, returned, base_flow[None, :], base_coupling, inverse, rim, wave_local, freq_local, sign_local)
    return jnp.transpose(marched.reshape(2, 5, local_modes, points), (2, 0, 1, 3))


def run(amplitudes, mode_table, slab_map, base_flow, base_coupling, slab_inverse, wall_operator):
    groups = lax.axis_size("modes")
    fits = (
        amplitudes.shape == (256, 2, 5, 512)
        and groups * SHARE == amplitudes.shape[3]
        and slab_inverse.shape == (8, 2 * SHARE, 2 * SHARE)
    )
    chosen = local_fast if fits else local
    return chosen(
        amplitudes, mode_table, slab_map, base_flow, base_coupling, slab_inverse, wall_operator
    )


def solution(mesh):
    return jax.shard_map(
        run,
        mesh=mesh,
        in_specs=(
            P(("runs", "modes"), None, None, None),
            P(),
            P(),
            P("runs"),
            P("runs", None),
            P(),
            P(),
        ),
        out_specs=P(("runs", "modes"), None, None, None),
        check_vma=False,
    )
```

```python
import functools
import math

import jax
import jax.numpy as jnp
import ml_dtypes
import numpy as np
from jax import lax
from jax.experimental import pallas as pl
from jax.experimental.pallas import tpu as pltpu
from jax.sharding import PartitionSpec as P

M = 4096
NB = 128
SWEEPS = 3
NW = 32


precise = lax.Precision.HIGHEST
omega_step = 0.01
phase_gain = 0.2
march_step = 0.2
coupling = 0.3


def twiddle(length):
    counter = jnp.arange(length, dtype=jnp.int32)
    product = counter[:, None] * counter[None, :] % length
    angles = product.astype(jnp.float32) * (2.0 * math.pi / length)
    return (jnp.cos(angles), jnp.sin(angles))


def mode_tables(mode_table):
    omega_index = mode_table[:, 0]
    beta_index = mode_table[:, 1]
    signed = jnp.where(beta_index >= NB // 2, beta_index - NB, beta_index)
    wavenum = 2.0 * signed.astype(jnp.float32) / NB
    frequency = omega_step * omega_index.astype(jnp.float32)
    grid_pos = omega_index * NB + beta_index
    mode_at = jnp.zeros((M,), jnp.int32).at[grid_pos].set(jnp.arange(M, dtype=jnp.int32))
    return (wavenum, frequency, grid_pos, mode_at)


def synthesize(real_part, imag_part, tables, factor):
    cos_omega, sin_omega, cos_beta, sin_beta = tables
    mixed_re = jnp.einsum("...wb,bz->...wz", real_part, cos_beta, precision=precise) - jnp.einsum(
        "...wb,bz->...wz", imag_part, sin_beta, precision=precise
    )
    mixed_im = jnp.einsum("...wb,bz->...wz", real_part, sin_beta, precision=precise) + jnp.einsum(
        "...wb,bz->...wz", imag_part, cos_beta, precision=precise
    )
    physical = jnp.einsum("...wz,wt->...tz", mixed_re, cos_omega, precision=precise) - jnp.einsum(
        "...wz,wt->...tz", mixed_im, sin_omega, precision=precise
    )
    return physical * factor


def analyze(physical, tables, factor):
    cos_omega, sin_omega, cos_beta, sin_beta = tables
    half_re = jnp.einsum("...tz,zb->...tb", physical, cos_beta, precision=precise)
    half_im = -jnp.einsum("...tz,zb->...tb", physical, sin_beta, precision=precise)
    coef_re = jnp.einsum("...tb,tw->...wb", half_re, cos_omega, precision=precise) + jnp.einsum(
        "...tb,tw->...wb", half_im, sin_omega, precision=precise
    )
    coef_im = jnp.einsum("...tb,tw->...wb", half_im, cos_omega, precision=precise) - jnp.einsum(
        "...tb,tw->...wb", half_re, sin_omega, precision=precise
    )
    return (coef_re * factor, coef_im * factor)


def forcing(normal_vel, spanwise_vel, wall_grad, span_grad, tables, factor):
    vel_v = synthesize(normal_vel[0], normal_vel[1], tables, factor)
    vel_w = synthesize(spanwise_vel[0], spanwise_vel[1], tables, factor)
    grad_y = synthesize(wall_grad[0], wall_grad[1], tables, factor)
    grad_z = synthesize(span_grad[0], span_grad[1], tables, factor)
    product = -(vel_v[None] * grad_y + vel_w[None] * grad_z)
    return analyze(product, tables, factor)


def wall_derivative(values, wall_operator):
    slab_width = wall_operator.shape[0]
    slab_count = values.shape[3] // slab_width
    blocks = values.reshape(values.shape[:3] + (slab_count, slab_width))
    return jnp.einsum("ij,abcsj->abcsi", wall_operator, blocks, precision=precise).reshape(
        values.shape
    )


def interface_table(slab_map, slab_count, slab_width):
    inverse = (
        jnp.zeros((slab_count,), jnp.int32)
        .at[slab_map]
        .set(jnp.arange(slab_count, dtype=jnp.int32))
    )
    position = jnp.arange(slab_count * slab_width, dtype=jnp.int32)
    slot_of = position // slab_width
    within = position % slab_width
    domain = inverse[slot_of]
    below = slab_map[jnp.maximum(domain - 1, 0)] * slab_width + (slab_width - 1)
    above = slab_map[jnp.minimum(domain + 1, slab_count - 1)] * slab_width
    lower_ok = (within == 0) & (domain > 0)
    upper_ok = (within == slab_width - 1) & (domain < slab_count - 1)
    source = jnp.where(lower_ok, below, jnp.where(upper_ok, above, 0))
    weight = (lower_ok | upper_ok).astype(jnp.float32)
    return (source, weight)


def relaxation(iterate, right_side, rotation, matrix, slab_inverse, source, weight):
    slab_count = slab_inverse.shape[0]
    slab_width = slab_inverse.shape[1]
    coupled = jnp.einsum("kjy,acjy->acky", matrix, iterate, precision=precise)
    applied = jnp.stack(
        [
            coupled[:, 0] - rotation[:, None, :] * iterate[:, 1],
            coupled[:, 1] + rotation[:, None, :] * iterate[:, 0],
        ],
        1,
    )
    rims = jnp.take(iterate, source, axis=3) * weight
    residual_in = right_side - applied + coupling * rims
    blocks = residual_in.reshape(iterate.shape[:3] + (slab_count, slab_width))
    return jnp.einsum("sij,acvsj->acvsi", slab_inverse, blocks, precision=precise).reshape(
        iterate.shape
    )


def local(amplitudes, mode_table, slab_map, base_flow, base_coupling, slab_inverse, wall_operator):
    local_modes = amplitudes.shape[0]
    wall_points = amplitudes.shape[3]
    groups = lax.axis_size("modes")
    point_share = wall_points // groups
    wavenum, frequency, grid_pos, mode_at = mode_tables(mode_table)
    first_mode = lax.axis_index("modes") * local_modes
    wave_local = lax.dynamic_slice_in_dim(wavenum, first_mode, local_modes)
    freq_local = lax.dynamic_slice_in_dim(frequency, first_mode, local_modes)
    tables = twiddle(NW) + twiddle(NB)
    factor = 1.0 / math.sqrt(M)
    source, weight = interface_table(slab_map, slab_inverse.shape[0], slab_inverse.shape[1])
    matrix = base_coupling.reshape(5, 5, wall_points)
    gradient = wall_derivative(amplitudes, wall_operator)
    span = jnp.stack(
        [
            -wave_local[:, None, None] * amplitudes[:, 1],
            wave_local[:, None, None] * amplitudes[:, 0],
        ],
        1,
    )
    fields = jnp.concatenate([amplitudes[:, :, 2:4], gradient, span], 2)
    field_count = fields.shape[2]
    channels = 2 * field_count
    outgoing = jnp.transpose(
        fields.reshape(local_modes, channels, groups, point_share), (1, 2, 3, 0)
    ).reshape(channels, groups, point_share * local_modes)
    incoming = lax.all_to_all(outgoing, "modes", split_axis=1, concat_axis=1, tiled=True)
    by_mode = jnp.transpose(
        incoming.reshape(channels, groups, point_share, local_modes), (0, 2, 1, 3)
    ).reshape(channels, point_share, M)
    gridded = by_mode[..., mode_at].reshape(2, field_count, point_share, NW, NB)
    normal_vel = gridded[:, 0]
    spanwise_vel = gridded[:, 1]
    wall_grad = gridded[:, 2:7]
    span_grad = gridded[:, 7:12]
    mean_crossflow = lax.all_gather(spanwise_vel[0, :, 0, 0], "modes", axis=0, tiled=True)
    coef_re, coef_im = forcing(normal_vel, spanwise_vel, wall_grad, span_grad, tables, factor)
    packed = jnp.stack([coef_re, coef_im], 0).reshape(10, point_share, M)[..., grid_pos]
    sendback = jnp.transpose(
        packed.reshape(10, point_share, groups, local_modes), (0, 2, 1, 3)
    ).reshape(10, groups, point_share * local_modes)
    returned = lax.all_to_all(sendback, "modes", split_axis=1, concat_axis=1, tiled=True)
    nonlinear = jnp.transpose(
        returned.reshape(10, groups, point_share, local_modes), (3, 0, 1, 2)
    ).reshape(local_modes, 2, 5, wall_points)
    crossflow = base_flow + mean_crossflow
    rotation = phase_gain * wave_local[:, None] * crossflow[None, :] - freq_local[:, None]
    right_side = amplitudes + march_step * nonlinear
    iterate = amplitudes
    for sweep_index in range(SWEEPS):
        iterate = relaxation(iterate, right_side, rotation, matrix, slab_inverse, source, weight)
    return iterate


F32 = jnp.float32
BF16 = jnp.bfloat16
VMEM_BYTES = 56 * 1024 * 1024
SHARE = 32
LANES = 128


def split_np(values):
    high = values.astype(np.float32).astype(ml_dtypes.bfloat16)
    low = (values - high.astype(np.float64)).astype(np.float32).astype(ml_dtypes.bfloat16)
    return high, low


def split(values):
    high = values.astype(BF16)
    low = (values - high.astype(F32)).astype(BF16)
    return high, low


def dot(left, right):
    return jnp.dot(left, right, preferred_element_type=F32)


def dot3(left, right):
    return dot(left[0], right[0]) + (dot(left[0], right[1]) + dot(left[1], right[0]))


def synthesis_matrix():
    index = np.arange(NB)
    angle = 2.0 * np.pi * (index[:, None] * index[None, :] % NB) / NB
    cos, sin = np.cos(angle), np.sin(angle)
    signed = np.where(index >= NB // 2, index - NB, index)
    wave = (2.0 * signed / NB)[None, :]
    rows = [
        np.concatenate([cos, -sin], 1),
        np.concatenate([sin, cos], 1),
        np.concatenate([-sin * wave, -cos * wave], 1),
        np.concatenate([cos * wave, -sin * wave], 1),
    ]
    return np.concatenate(rows, 0) / math.sqrt(M)


def analysis_matrix():
    index = np.arange(NB)
    angle = 2.0 * np.pi * (index[:, None] * index[None, :] % NB) / NB
    cos, sin = np.cos(angle), np.sin(angle)
    rows = [np.concatenate([cos, sin], 1), np.concatenate([-sin, cos], 1)]
    return np.concatenate(rows, 0) / math.sqrt(M)


def weighted(terms, weights):
    total = None
    for term, weight in zip(terms, weights):
        if abs(weight) < 1e-12:
            continue
        if abs(weight - 1.0) < 1e-12:
            part = term
        elif abs(weight + 1.0) < 1e-12:
            part = -term
        else:
            part = term * np.float32(weight)
        total = part if total is None else total + part
    return total


def cosine_sums(terms):
    half, quarter = NW // 2, NW // 4
    out = [None] * (half + 1)
    for t in range(quarter + 1):
        even = weighted(terms[0::2], [math.cos(2 * math.pi * w * t / NW) for w in range(0, half + 1, 2)])
        odd = weighted(terms[1::2], [math.cos(2 * math.pi * w * t / NW) for w in range(1, half + 1, 2)])
        if odd is None:
            out[t] = even
            out[half - t] = even
        else:
            out[t] = even + odd
            out[half - t] = even - odd
    return out


def sine_sums(terms):
    half, quarter = NW // 2, NW // 4
    out = [None] * half
    for t in range(1, quarter + 1):
        even = weighted(terms[2::2], [math.sin(2 * math.pi * w * t / NW) for w in range(2, half, 2)])
        odd = weighted(terms[1::2], [math.sin(2 * math.pi * w * t / NW) for w in range(1, half, 2)])
        if even is None:
            out[t] = odd
        else:
            out[t] = odd + even
            out[half - t] = odd - even
    return out


def lane_group(shape):
    return lax.broadcasted_iota(jnp.int32, shape, len(shape) - 1) // SHARE


def shifted(values, groups):
    groups = groups % 4
    return values if groups == 0 else pltpu.roll(values, groups * SHARE, values.ndim - 1)


def join(pieces, which):
    low = jnp.where(which == 0, pieces[0], pieces[1])
    high = jnp.where(which == 2, pieces[2], pieces[3])
    return jnp.where(which < 2, low, high)


def halves(first, second, wide):
    return jnp.where(wide, first, shifted(second, 2))


def pack_first_kernel(amp_ref, out_ref):
    which = lane_group((8, LANES))

    def body(step, carry):
        rows = pl.ds(pl.multiple_of(step * 8, 8), 8)
        for tile in range(4):
            parts = [amp_ref[c, rows, tile * LANES : (tile + 1) * LANES] for c in (2, 3, 7, 8)]
            for q in range(4):
                out_ref[tile * 4 + q, rows, :] = join([shifted(parts[k], k - q) for k in range(4)], which)
        return carry

    lax.fori_loop(0, amp_ref.shape[1] // 8, body, 0)


def pack_second_kernel(amp_ref, out_ref):
    half = amp_ref.shape[1] // 2
    full = 2 * half
    which = lane_group((8, LANES))

    def body(step, carry):
        row = pl.multiple_of(step * 8, 8)
        for tile in range(4):
            lanes = slice(tile * LANES, (tile + 1) * LANES)
            rest = []
            for side in range(2):
                rows = pl.ds(row + side * half, 8)
                parts = [amp_ref[c, rows, lanes] for c in (0, 1, 5, 6)]
                rest += [amp_ref[c, rows, lanes] for c in (4, 9)]
                for q in range(4):
                    out_ref[tile * 4 + q, rows, :] = join([shifted(parts[k], k - q) for k in range(4)], which)
            for q in range(4):
                out_ref[tile * 4 + q, pl.ds(row + full, 8), :] = join(
                    [shifted(rest[k], k - q) for k in range(4)], which
                )
        return carry

    lax.fori_loop(0, half // 8, body, 0)


def physical_kernel(with_rest, pos_ref, in_ref, high_ref, low_ref, field_ref, span_ref, mean_ref, ga, gc, mid):
    sources = in_ref.shape[0]
    full = M // sources
    half = full // 2

    def spread(source, carry):
        def rows_of(step, inner):
            row = pl.multiple_of(step * 8, 8)
            if with_rest:
                rest = in_ref[source, pl.ds(row + full, 8), :]
            for side in range(2):
                first = row + side * half
                a8 = in_ref[source, pl.ds(first, 8), :]
                if with_rest:
                    c8 = shifted(rest, 2 * side)
                for u in range(8):
                    where = pos_ref[source * full + first + u]
                    ga[pl.ds(where, 1), :] = a8[u : u + 1, :]
                    if with_rest:
                        gc[pl.ds(where, 1), :] = c8[u : u + 1, :]
            return inner

        return lax.fori_loop(0, half // 8, rows_of, carry)

    lax.fori_loop(0, sources, spread, 0)
    mean_ref[...] = jnp.broadcast_to(ga[0:1, :], mean_ref.shape)

    tall = lane_group((NB, LANES))

    def store(omega, group, out, count):
        for part in range(2):
            mid[omega, (2 * group + part) * NB : (2 * group + part + 1) * NB, :] = jnp.where(
                tall < count,
                out[part * NB : (part + 1) * NB],
                shifted(out[(2 + part) * NB : (3 + part) * NB], count),
            )

    def beta_sum(step, carry):
        if with_rest:
            rows = pl.ds(pl.multiple_of(step * NB, NB), NB)
            first, second, turn = ga[rows, :], gc[rows, :], 3
        else:
            first = ga[pl.ds(pl.multiple_of(step * 2 * NB, NB), NB), :]
            second, turn = ga[pl.ds(pl.multiple_of(step * 2 * NB + NB, NB), NB), :], 2
        data = jnp.concatenate(
            [
                jnp.concatenate([first, second], 1),
                jnp.concatenate([shifted(first, 2), shifted(second, turn)], 1),
            ],
            0,
        )
        out = dot3((high_ref[...], low_ref[...]), split(data))
        if with_rest:
            store(step, 0, out[:, :LANES], 2)
            store(step, 1, out[:, LANES:], 1)
        else:
            store(2 * step, 0, out[:, :LANES], 2)
            store(2 * step + 1, 0, out[:, LANES:], 2)
        return carry

    lax.fori_loop(0, NW if with_rest else NW // 2, beta_sum, 0)

    which = lane_group((8, LANES))
    half_w = NW // 2

    def omega_sum(step, carry):
        row = pl.multiple_of(step * 8, 8)
        rows = pl.ds(row, 8)
        for group in range(2 if with_rest else 1):
            re = [mid[w, pl.ds(row + 2 * group * NB, 8), :] for w in range(NW)]
            im = [mid[w, pl.ds(row + (2 * group + 1) * NB, 8), :] for w in range(NW)]
            cos_terms = [re[0]] + [re[w] + re[NW - w] for w in range(1, half_w)] + [re[half_w]]
            sin_terms = [None] + [im[w] - im[NW - w] for w in range(1, half_w)]
            even = cosine_sums(cos_terms)
            odd = sine_sums(sin_terms)
            out = [None] * NW
            out[0] = even[0]
            out[half_w] = even[half_w]
            for t in range(1, half_w):
                out[t] = even[t] - odd[t]
                out[NW - t] = even[t] + odd[t]
            if group == 0:
                for t in range(half_w):
                    field_ref[t, rows, :] = halves(out[t], out[t + half_w], which < 2)
                    span_ref[t, rows, :] = jnp.where(which < 2, shifted(out[t], 2), out[t + half_w])
            else:
                for t in range(8):
                    for target, start in ((field_ref, 0), (span_ref, 1)):
                        target[half_w + t, rows, :] = join(
                            [shifted(out[t + 8 * k], k - start) for k in range(4)], which
                        )
        return carry

    lax.fori_loop(0, NB // 8, omega_sum, 0)


def force_kernel(
    with_rest, pos_ref, flow_ref, field_ref, other_ref, span_ref, mean_ref, wall_ref, high_ref, low_ref,
    out_ref, force, mid, na, nc, rest_rows,
):
    sources = out_ref.shape[0]
    full = M // sources
    half = full // 2
    wall = split(wall_ref[...])
    half_w = NW // 2
    tall = lane_group((NB, LANES))
    is_even = (tall % 2) == 0

    def products(step, carry):
        def one(row, v, w):
            both = jnp.concatenate([field_ref[row], other_ref[row]], 1)
            force[row] = -(v * dot3(split(both), wall) + w * span_ref[row])

        pair = [flow_ref[step], flow_ref[step + 8]]
        for k in range(2):
            one(
                step + 8 * k,
                jnp.where(is_even, pair[k], shifted(pair[k], 1)),
                jnp.where(is_even, shifted(pair[k], 3), pair[k]),
            )
        if with_rest:
            one(
                step + half_w,
                jnp.where(is_even, pair[0], shifted(pair[1], 1)),
                jnp.where(is_even, shifted(pair[0], 3), pair[1]),
            )
        return carry

    lax.fori_loop(0, 8, products, 0)

    def time_sum(step, carry):
        row = pl.multiple_of(step * 8, 8)
        rows = pl.ds(row, 8)
        for group in range(2 if with_rest else 1):
            if group == 0:
                packed = [force[t, rows, :] for t in range(half_w)]
                values = packed + [shifted(value, 2) for value in packed]
            else:
                packed = [force[half_w + t, rows, :] for t in range(8)]
                values = [shifted(packed[t % 8], -(t // 8)) for t in range(NW)]
            cos_terms = (
                [values[0]]
                + [values[t] + values[NW - t] for t in range(1, half_w)]
                + [values[half_w]]
            )
            sin_terms = [None] + [values[NW - t] - values[t] for t in range(1, half_w)]
            even = cosine_sums(cos_terms)
            odd = sine_sums(sin_terms)
            lanes = slice(group * LANES, (group + 1) * LANES)
            zero = jnp.zeros((8, LANES), F32)
            for w in range(half_w + 1):
                mid[w, rows, lanes] = even[w]
                mid[w, pl.ds(row + NB, 8), lanes] = odd[w] if 0 < w < half_w else zero
        return carry

    lax.fori_loop(0, NB // 8, time_sum, 0)

    def span_sum(omega, carry):
        out = dot3((high_ref[...], low_ref[...]), split(mid[omega]))
        rows = pl.ds(pl.multiple_of(omega * NB, NB), NB)
        na[rows, :] = halves(out[:NB, :LANES], out[NB:, :LANES], tall < 2)
        if with_rest:
            nc[rows, :] = jnp.where(tall < 1, out[:NB, LANES:], shifted(out[NB:, LANES:], 1))
        return carry

    lax.fori_loop(0, half_w + 1, span_sum, 0)

    def collect(source, carry):
        def rows_of(step, inner):
            row = pl.multiple_of(step * 8, 8)
            for side in range(2):
                first = row + side * half
                for u in range(8):
                    where = pos_ref[source * full + first + u]
                    out_ref[source, pl.ds(first + u, 1), :] = na[pl.ds(where, 1), :]
                    if with_rest:
                        rest_rows[side, pl.ds(row + u, 1), :] = nc[pl.ds(where, 1), :]
            return inner

        lax.fori_loop(0, half // 8, rows_of, 0)
        if with_rest:
            out_ref[source, full : full + half, :] = halves(
                rest_rows[0], rest_rows[1], lane_group((half, LANES)) < 2
            )
        else:
            out_ref[source, full : full + 8, :] = mean_ref[...]
        return carry

    lax.fori_loop(0, sources, collect, 0)


def sweep_kernel(
    amp_ref, first_ref, second_ref, base_ref, matrix_ref, inverse_ref, rim_ref, wave_ref, freq_ref, sign_ref,
    out_ref, right, current, residual, flow,
):
    half = amp_ref.shape[1] // 2
    full = 2 * half
    rows_in = 16
    which = lane_group((rows_in, LANES))
    which8 = lane_group((8, LANES))
    for tile in range(4):
        mean = join([shifted(first_ref[4 * tile + k, full : full + 8, :], k - 1) for k in range(4)], which8)
        flow[:, tile * LANES : (tile + 1) * LANES] = mean + base_ref[:, tile * LANES : (tile + 1) * LANES]
    inverse = [split(inverse_ref[g]) for g in range(2)]

    def chunk(step, carry):
        row = pl.multiple_of(step * rows_in, rows_in)
        for tile in range(4):
            lanes = slice(tile * LANES, (tile + 1) * LANES)
            rest = [second_ref[4 * tile + k, pl.ds(row + full, rows_in), :] for k in range(4)]
            for side in range(2):
                rows = pl.ds(row + side * half, rows_in)
                sign = sign_ref[rows, :]
                got = [
                    [ref[4 * tile + k, rows, :] for k in range(4)] for ref in (second_ref, first_ref)
                ]
                for part in range(2):
                    for c in range(5):
                        if c < 4:
                            source, place = got[c // 2], 2 * part + c % 2
                        else:
                            source, place = rest, 2 * side + part
                        value = join([shifted(source[k], k - place) for k in range(4)], which)
                        if part == 1:
                            value = value * sign
                        own = amp_ref[5 * part + c, rows, lanes]
                        place = slice((5 * part + c) * 32 + side * 16, (5 * part + c) * 32 + side * 16 + 16)
                        current[place, lanes] = own
                        right[place, lanes] = own + march_step * value

        for sweep in range(SWEEPS):
            high, low = split(current[...])
            residual[...] = right[...] + coupling * (dot(high, rim_ref[...]) + dot(low, rim_ref[...]))
            for tile in range(4):
                lanes = slice(tile * LANES, (tile + 1) * LANES)
                for side in range(2):
                    rows = pl.ds(row + side * half, rows_in)
                    rotation = phase_gain * wave_ref[rows, :] * flow[0:1, lanes] - freq_ref[rows, :]
                    x = [current[c * 32 + side * 16 : c * 32 + side * 16 + 16, lanes] for c in range(10)]
                    for part in range(2):
                        for c in range(5):
                            total = rotation * x[5 * (1 - part) + c]
                            if part == 0:
                                total = -total
                            for j in range(5):
                                total = total + matrix_ref[5 * c + j : 5 * c + j + 1, lanes] * x[5 * part + j]
                            place = slice((5 * part + c) * 32 + side * 16, (5 * part + c) * 32 + side * 16 + 16)
                            residual[place, lanes] = residual[place, lanes] - total
            for g in range(2):
                lanes = slice(g * 256, (g + 1) * 256)
                current[:, lanes] = dot3(split(residual[:, lanes]), inverse[g])
        for c in range(10):
            for side in range(2):
                out_ref[c, pl.ds(row + side * half, rows_in), :] = current[
                    c * 32 + side * 16 : c * 32 + side * 16 + 16, :
                ]
        return carry

    lax.fori_loop(0, half // rows_in, chunk, 0)


def local_fast(amplitudes, mode_table, slab_map, base_flow, base_coupling, slab_inverse, wall_operator):
    local_modes = amplitudes.shape[0]
    points = amplitudes.shape[3]
    groups = lax.axis_size("modes")
    me = lax.axis_index("modes")
    half = local_modes // 2
    vmem = pl.BlockSpec(memory_space=pltpu.VMEM)
    smem = pl.BlockSpec(memory_space=pltpu.SMEM)
    params = pltpu.CompilerParams(vmem_limit_bytes=VMEM_BYTES)
    width = slab_inverse.shape[1]

    def cost(micros):
        return pl.CostEstimate(flops=micros * 10**9, bytes_accessed=micros * 3 * 10**6, transcendentals=0)


    omega_index = mode_table[:, 0]
    beta_index = mode_table[:, 1]
    grid_pos = omega_index * NB + beta_index
    mirrored = omega_index > NW // 2
    back_pos = jnp.where(mirrored, (NW - omega_index) * NB + (NB - beta_index) % NB, grid_pos)
    local_table = lax.dynamic_slice_in_dim(mode_table, me * local_modes, local_modes)
    omega_local = local_table[:, 0:1]
    beta_local = local_table[:, 1:2]
    signed = jnp.where(beta_local >= NB // 2, beta_local - NB, beta_local)
    wave_local = 2.0 * signed.astype(F32) / NB
    freq_local = omega_step * omega_local.astype(F32)
    sign_local = jnp.where(omega_local > NW // 2, -1.0, 1.0).astype(F32)

    part = lax.rem(me, 2) * SHARE
    rows = lax.dynamic_slice_in_dim(wall_operator, part, SHARE, 0)
    mine = lax.dynamic_slice_in_dim(rows, part, SHARE, 1)
    theirs = lax.dynamic_slice_in_dim(rows, SHARE - part, SHARE, 1)
    eye = jnp.eye(4, dtype=F32)

    def blocks(value):
        size = value.shape[0]
        return (eye[:, None, :, None] * value.T[None, :, None, :]).reshape(4 * size, 4 * size)

    wall = jnp.concatenate([blocks(mine), blocks(theirs)], 0)
    turned = jnp.swapaxes(slab_inverse, 1, 2).reshape(2, 4, width, 1, width)
    inverse = (turned * eye[None, :, None, :, None]).reshape(2, 4 * width, 4 * width)
    source, weight = interface_table(slab_map, slab_inverse.shape[0], width)
    rim = ((jnp.arange(points, dtype=jnp.int32)[:, None] == source[None, :]) & (weight[None, :] > 0)).astype(BF16)

    amp = jnp.transpose(amplitudes, (1, 2, 0, 3)).reshape(10, local_modes, points)
    synthesis = [jnp.asarray(part) for part in split_np(synthesis_matrix())]
    analysis = [jnp.asarray(part) for part in split_np(analysis_matrix())]
    half_w = NW // 2
    rows_back = (half_w + 1) * NB

    def pack(kernel, source, rows, name):
        return pl.pallas_call(
            kernel,
            out_shape=jax.ShapeDtypeStruct((groups, rows, LANES), F32),
            in_specs=[vmem],
            out_specs=vmem,
            compiler_params=params,
            cost_estimate=cost(6),
            name=name,
        )(source)

    def exchange(message):
        return lax.all_to_all(message, "modes", split_axis=0, concat_axis=0, tiled=True)

    def physical(arrived, with_rest):
        count = half_w + (8 if with_rest else 0)
        block = jax.ShapeDtypeStruct((count, NB, LANES), F32)
        kinds = 2 if with_rest else 1
        return pl.pallas_call(
            functools.partial(physical_kernel, with_rest),
            out_shape=[block, block, jax.ShapeDtypeStruct((8, LANES), F32)],
            in_specs=[smem, vmem, vmem, vmem],
            out_specs=[vmem, vmem, vmem],
            scratch_shapes=[
                pltpu.VMEM((M, LANES), F32),
                pltpu.VMEM((M if with_rest else 8, LANES), F32),
                pltpu.VMEM((NW, 2 * kinds * NB, LANES), F32),
            ],
            compiler_params=params,
            cost_estimate=cost(15 * kinds),
            name="physical" + str(kinds),
        )(grid_pos, arrived, *synthesis)

    def swap(field):
        return lax.ppermute(field, "modes", [(i, i ^ 1) for i in range(groups)])

    def forces(flow, field, other, span, mean, with_rest):
        kinds = 2 if with_rest else 1
        return pl.pallas_call(
            functools.partial(force_kernel, with_rest),
            out_shape=jax.ShapeDtypeStruct((groups, 3 * half if with_rest else 2 * half + 8, LANES), F32),
            in_specs=[smem] + [vmem] * 8,
            out_specs=vmem,
            scratch_shapes=[
                pltpu.VMEM((half_w + 8, NB, LANES), F32),
                pltpu.VMEM((half_w + 1, 2 * NB, kinds * LANES), F32),
                pltpu.VMEM((rows_back, LANES), F32),
                pltpu.VMEM((rows_back if with_rest else 8, LANES), F32),
                pltpu.VMEM((2, half, LANES), F32),
            ],
            compiler_params=params,
            cost_estimate=cost(10 * kinds),
            name="force" + str(kinds),
        )(back_pos, flow, field, other, span, mean, wall, *analysis)

    first_message = pack(pack_first_kernel, amp, 2 * half, "pack1")
    first_message, later = lax.optimization_barrier((first_message, amp))
    first = exchange(first_message)
    second_message = pack(pack_second_kernel, later, 3 * half, "pack2")
    second = exchange(second_message)
    first, second_message = lax.optimization_barrier((first, second_message))
    flow, flow_span, mean = physical(first, False)
    first_force = forces(flow, flow, swap(flow), flow_span, mean, False)
    first_force, second = lax.optimization_barrier((first_force, second))
    first_back = exchange(first_force)
    field, span, unused = physical(second, True)
    second_back = exchange(forces(flow, field, swap(field), span, unused, True))

    marched = pl.pallas_call(
        sweep_kernel,
        out_shape=jax.ShapeDtypeStruct((10, local_modes, points), F32),
        in_specs=[vmem] * 10,
        out_specs=vmem,
        scratch_shapes=[pltpu.VMEM((320, points), F32)] * 3 + [pltpu.VMEM((8, points), F32)],
        compiler_params=params,
        name="sweeps",
    )(amp, first_back, second_back, base_flow[None, :], base_coupling, inverse, rim, wave_local, freq_local, sign_local)
    return jnp.transpose(marched.reshape(2, 5, local_modes, points), (2, 0, 1, 3))


def run(amplitudes, mode_table, slab_map, base_flow, base_coupling, slab_inverse, wall_operator):
    groups = lax.axis_size("modes")
    fits = (
        amplitudes.shape == (256, 2, 5, 512)
        and groups * SHARE == amplitudes.shape[3]
        and slab_inverse.shape == (8, 2 * SHARE, 2 * SHARE)
    )
    chosen = local_fast if fits else local
    return chosen(
        amplitudes, mode_table, slab_map, base_flow, base_coupling, slab_inverse, wall_operator
    )


def solution(mesh):
    return jax.shard_map(
        run,
        mesh=mesh,
        in_specs=(
            P(("runs", "modes"), None, None, None),
            P(),
            P(),
            P("runs"),
            P("runs", None),
            P(),
            P(),
        ),
        out_specs=P(("runs", "modes"), None, None, None),
        check_vma=False,
    )
```

```python
import functools
import math

import jax
import jax.numpy as jnp
import ml_dtypes
import numpy as np
from jax import lax
from jax.experimental import pallas as pl
from jax.experimental.pallas import tpu as pltpu
from jax.sharding import PartitionSpec as P

M = 4096
NB = 128
SWEEPS = 3
NW = 32


precise = lax.Precision.HIGHEST
omega_step = 0.01
phase_gain = 0.2
march_step = 0.2
coupling = 0.3


def twiddle(length):
    counter = jnp.arange(length, dtype=jnp.int32)
    product = counter[:, None] * counter[None, :] % length
    angles = product.astype(jnp.float32) * (2.0 * math.pi / length)
    return (jnp.cos(angles), jnp.sin(angles))


def mode_tables(mode_table):
    omega_index = mode_table[:, 0]
    beta_index = mode_table[:, 1]
    signed = jnp.where(beta_index >= NB // 2, beta_index - NB, beta_index)
    wavenum = 2.0 * signed.astype(jnp.float32) / NB
    frequency = omega_step * omega_index.astype(jnp.float32)
    grid_pos = omega_index * NB + beta_index
    mode_at = jnp.zeros((M,), jnp.int32).at[grid_pos].set(jnp.arange(M, dtype=jnp.int32))
    return (wavenum, frequency, grid_pos, mode_at)


def synthesize(real_part, imag_part, tables, factor):
    cos_omega, sin_omega, cos_beta, sin_beta = tables
    mixed_re = jnp.einsum("...wb,bz->...wz", real_part, cos_beta, precision=precise) - jnp.einsum(
        "...wb,bz->...wz", imag_part, sin_beta, precision=precise
    )
    mixed_im = jnp.einsum("...wb,bz->...wz", real_part, sin_beta, precision=precise) + jnp.einsum(
        "...wb,bz->...wz", imag_part, cos_beta, precision=precise
    )
    physical = jnp.einsum("...wz,wt->...tz", mixed_re, cos_omega, precision=precise) - jnp.einsum(
        "...wz,wt->...tz", mixed_im, sin_omega, precision=precise
    )
    return physical * factor


def analyze(physical, tables, factor):
    cos_omega, sin_omega, cos_beta, sin_beta = tables
    half_re = jnp.einsum("...tz,zb->...tb", physical, cos_beta, precision=precise)
    half_im = -jnp.einsum("...tz,zb->...tb", physical, sin_beta, precision=precise)
    coef_re = jnp.einsum("...tb,tw->...wb", half_re, cos_omega, precision=precise) + jnp.einsum(
        "...tb,tw->...wb", half_im, sin_omega, precision=precise
    )
    coef_im = jnp.einsum("...tb,tw->...wb", half_im, cos_omega, precision=precise) - jnp.einsum(
        "...tb,tw->...wb", half_re, sin_omega, precision=precise
    )
    return (coef_re * factor, coef_im * factor)


def forcing(normal_vel, spanwise_vel, wall_grad, span_grad, tables, factor):
    vel_v = synthesize(normal_vel[0], normal_vel[1], tables, factor)
    vel_w = synthesize(spanwise_vel[0], spanwise_vel[1], tables, factor)
    grad_y = synthesize(wall_grad[0], wall_grad[1], tables, factor)
    grad_z = synthesize(span_grad[0], span_grad[1], tables, factor)
    product = -(vel_v[None] * grad_y + vel_w[None] * grad_z)
    return analyze(product, tables, factor)


def wall_derivative(values, wall_operator):
    slab_width = wall_operator.shape[0]
    slab_count = values.shape[3] // slab_width
    blocks = values.reshape(values.shape[:3] + (slab_count, slab_width))
    return jnp.einsum("ij,abcsj->abcsi", wall_operator, blocks, precision=precise).reshape(
        values.shape
    )


def interface_table(slab_map, slab_count, slab_width):
    inverse = (
        jnp.zeros((slab_count,), jnp.int32)
        .at[slab_map]
        .set(jnp.arange(slab_count, dtype=jnp.int32))
    )
    position = jnp.arange(slab_count * slab_width, dtype=jnp.int32)
    slot_of = position // slab_width
    within = position % slab_width
    domain = inverse[slot_of]
    below = slab_map[jnp.maximum(domain - 1, 0)] * slab_width + (slab_width - 1)
    above = slab_map[jnp.minimum(domain + 1, slab_count - 1)] * slab_width
    lower_ok = (within == 0) & (domain > 0)
    upper_ok = (within == slab_width - 1) & (domain < slab_count - 1)
    source = jnp.where(lower_ok, below, jnp.where(upper_ok, above, 0))
    weight = (lower_ok | upper_ok).astype(jnp.float32)
    return (source, weight)


def relaxation(iterate, right_side, rotation, matrix, slab_inverse, source, weight):
    slab_count = slab_inverse.shape[0]
    slab_width = slab_inverse.shape[1]
    coupled = jnp.einsum("kjy,acjy->acky", matrix, iterate, precision=precise)
    applied = jnp.stack(
        [
            coupled[:, 0] - rotation[:, None, :] * iterate[:, 1],
            coupled[:, 1] + rotation[:, None, :] * iterate[:, 0],
        ],
        1,
    )
    rims = jnp.take(iterate, source, axis=3) * weight
    residual_in = right_side - applied + coupling * rims
    blocks = residual_in.reshape(iterate.shape[:3] + (slab_count, slab_width))
    return jnp.einsum("sij,acvsj->acvsi", slab_inverse, blocks, precision=precise).reshape(
        iterate.shape
    )


def local(amplitudes, mode_table, slab_map, base_flow, base_coupling, slab_inverse, wall_operator):
    local_modes = amplitudes.shape[0]
    wall_points = amplitudes.shape[3]
    groups = lax.axis_size("modes")
    point_share = wall_points // groups
    wavenum, frequency, grid_pos, mode_at = mode_tables(mode_table)
    first_mode = lax.axis_index("modes") * local_modes
    wave_local = lax.dynamic_slice_in_dim(wavenum, first_mode, local_modes)
    freq_local = lax.dynamic_slice_in_dim(frequency, first_mode, local_modes)
    tables = twiddle(NW) + twiddle(NB)
    factor = 1.0 / math.sqrt(M)
    source, weight = interface_table(slab_map, slab_inverse.shape[0], slab_inverse.shape[1])
    matrix = base_coupling.reshape(5, 5, wall_points)
    gradient = wall_derivative(amplitudes, wall_operator)
    span = jnp.stack(
        [
            -wave_local[:, None, None] * amplitudes[:, 1],
            wave_local[:, None, None] * amplitudes[:, 0],
        ],
        1,
    )
    fields = jnp.concatenate([amplitudes[:, :, 2:4], gradient, span], 2)
    field_count = fields.shape[2]
    channels = 2 * field_count
    outgoing = jnp.transpose(
        fields.reshape(local_modes, channels, groups, point_share), (1, 2, 3, 0)
    ).reshape(channels, groups, point_share * local_modes)
    incoming = lax.all_to_all(outgoing, "modes", split_axis=1, concat_axis=1, tiled=True)
    by_mode = jnp.transpose(
        incoming.reshape(channels, groups, point_share, local_modes), (0, 2, 1, 3)
    ).reshape(channels, point_share, M)
    gridded = by_mode[..., mode_at].reshape(2, field_count, point_share, NW, NB)
    normal_vel = gridded[:, 0]
    spanwise_vel = gridded[:, 1]
    wall_grad = gridded[:, 2:7]
    span_grad = gridded[:, 7:12]
    mean_crossflow = lax.all_gather(spanwise_vel[0, :, 0, 0], "modes", axis=0, tiled=True)
    coef_re, coef_im = forcing(normal_vel, spanwise_vel, wall_grad, span_grad, tables, factor)
    packed = jnp.stack([coef_re, coef_im], 0).reshape(10, point_share, M)[..., grid_pos]
    sendback = jnp.transpose(
        packed.reshape(10, point_share, groups, local_modes), (0, 2, 1, 3)
    ).reshape(10, groups, point_share * local_modes)
    returned = lax.all_to_all(sendback, "modes", split_axis=1, concat_axis=1, tiled=True)
    nonlinear = jnp.transpose(
        returned.reshape(10, groups, point_share, local_modes), (3, 0, 1, 2)
    ).reshape(local_modes, 2, 5, wall_points)
    crossflow = base_flow + mean_crossflow
    rotation = phase_gain * wave_local[:, None] * crossflow[None, :] - freq_local[:, None]
    right_side = amplitudes + march_step * nonlinear
    iterate = amplitudes
    for sweep_index in range(SWEEPS):
        iterate = relaxation(iterate, right_side, rotation, matrix, slab_inverse, source, weight)
    return iterate


F32 = jnp.float32
BF16 = jnp.bfloat16
VMEM_BYTES = 56 * 1024 * 1024
SHARE = 32
LANES = 128


def split_np(values):
    high = values.astype(np.float32).astype(ml_dtypes.bfloat16)
    low = (values - high.astype(np.float64)).astype(np.float32).astype(ml_dtypes.bfloat16)
    return high, low


def split(values):
    high = values.astype(BF16)
    low = (values - high.astype(F32)).astype(BF16)
    return high, low


def dot(left, right):
    return jnp.dot(left, right, preferred_element_type=F32)


def dot3(left, right):
    return dot(left[0], right[0]) + (dot(left[0], right[1]) + dot(left[1], right[0]))


def synthesis_matrix():
    index = np.arange(NB)
    angle = 2.0 * np.pi * (index[:, None] * index[None, :] % NB) / NB
    cos, sin = np.cos(angle), np.sin(angle)
    signed = np.where(index >= NB // 2, index - NB, index)
    wave = (2.0 * signed / NB)[None, :]
    rows = [
        np.concatenate([cos, -sin], 1),
        np.concatenate([sin, cos], 1),
        np.concatenate([-sin * wave, -cos * wave], 1),
        np.concatenate([cos * wave, -sin * wave], 1),
    ]
    return np.concatenate(rows, 0) / math.sqrt(M)


def analysis_matrix():
    index = np.arange(NB)
    angle = 2.0 * np.pi * (index[:, None] * index[None, :] % NB) / NB
    cos, sin = np.cos(angle), np.sin(angle)
    rows = [np.concatenate([cos, sin], 1), np.concatenate([-sin, cos], 1)]
    return np.concatenate(rows, 0) / math.sqrt(M)


def weighted(terms, weights):
    total = None
    for term, weight in zip(terms, weights):
        if abs(weight) < 1e-12:
            continue
        if abs(weight - 1.0) < 1e-12:
            part = term
        elif abs(weight + 1.0) < 1e-12:
            part = -term
        else:
            part = term * np.float32(weight)
        total = part if total is None else total + part
    return total


def cosine_sums(terms):
    half, quarter = NW // 2, NW // 4
    out = [None] * (half + 1)
    for t in range(quarter + 1):
        even = weighted(terms[0::2], [math.cos(2 * math.pi * w * t / NW) for w in range(0, half + 1, 2)])
        odd = weighted(terms[1::2], [math.cos(2 * math.pi * w * t / NW) for w in range(1, half + 1, 2)])
        if odd is None:
            out[t] = even
            out[half - t] = even
        else:
            out[t] = even + odd
            out[half - t] = even - odd
    return out


def sine_sums(terms):
    half, quarter = NW // 2, NW // 4
    out = [None] * half
    for t in range(1, quarter + 1):
        even = weighted(terms[2::2], [math.sin(2 * math.pi * w * t / NW) for w in range(2, half, 2)])
        odd = weighted(terms[1::2], [math.sin(2 * math.pi * w * t / NW) for w in range(1, half, 2)])
        if even is None:
            out[t] = odd
        else:
            out[t] = odd + even
            out[half - t] = odd - even
    return out


def lane_group(shape):
    return lax.broadcasted_iota(jnp.int32, shape, len(shape) - 1) // SHARE


def shifted(values, groups):
    groups = groups % 4
    return values if groups == 0 else pltpu.roll(values, groups * SHARE, values.ndim - 1)


def join(pieces, which):
    low = jnp.where(which == 0, pieces[0], pieces[1])
    high = jnp.where(which == 2, pieces[2], pieces[3])
    return jnp.where(which < 2, low, high)


def halves(first, second, wide):
    return jnp.where(wide, first, shifted(second, 2))


def channel(amp_ref, c, row, count, tile):
    return amp_ref[pl.ds(row * 40 + (c % 5) * 8 + tile * 2 + c // 5, count, stride=40), :]


def pack_first_kernel(amp_ref, out_ref):
    which = lane_group((8, LANES))

    def body(step, carry):
        row = pl.multiple_of(step * 8, 8)
        rows = pl.ds(row, 8)
        for tile in range(4):
            parts = [channel(amp_ref, c, row, 8, tile) for c in (2, 3, 7, 8)]
            for q in range(4):
                out_ref[tile * 4 + q, rows, :] = join([shifted(parts[k], k - q) for k in range(4)], which)
        return carry

    lax.fori_loop(0, amp_ref.shape[0] // 320, body, 0)


def pack_second_kernel(amp_ref, out_ref):
    half = amp_ref.shape[0] // 80
    full = 2 * half
    which = lane_group((8, LANES))

    def body(step, carry):
        row = pl.multiple_of(step * 8, 8)
        for tile in range(4):
            rest = []
            for side in range(2):
                rows = pl.ds(row + side * half, 8)
                parts = [channel(amp_ref, c, row + side * half, 8, tile) for c in (0, 1, 5, 6)]
                rest += [channel(amp_ref, c, row + side * half, 8, tile) for c in (4, 9)]
                for q in range(4):
                    out_ref[tile * 4 + q, rows, :] = join([shifted(parts[k], k - q) for k in range(4)], which)
            for q in range(4):
                out_ref[tile * 4 + q, pl.ds(row + full, 8), :] = join(
                    [shifted(rest[k], k - q) for k in range(4)], which
                )
        return carry

    lax.fori_loop(0, half // 8, body, 0)


def physical_kernel(with_rest, pos_ref, in_ref, high_ref, low_ref, field_ref, span_ref, mean_ref, ga, gc, mid):
    sources = in_ref.shape[0]
    full = M // sources
    half = full // 2

    def spread(source, carry):
        def rows_of(step, inner):
            row = pl.multiple_of(step * 8, 8)
            if with_rest:
                rest = in_ref[source, pl.ds(row + full, 8), :]
            for side in range(2):
                first = row + side * half
                a8 = in_ref[source, pl.ds(first, 8), :]
                if with_rest:
                    c8 = shifted(rest, 2 * side)
                for u in range(8):
                    where = pos_ref[source * full + first + u]
                    ga[pl.ds(where, 1), :] = a8[u : u + 1, :]
                    if with_rest:
                        gc[pl.ds(where, 1), :] = c8[u : u + 1, :]
            return inner

        return lax.fori_loop(0, half // 8, rows_of, carry)

    lax.fori_loop(0, sources, spread, 0)
    mean_ref[...] = jnp.broadcast_to(ga[0:1, :], mean_ref.shape)

    tall = lane_group((NB, LANES))

    def store(omega, group, out, count):
        for part in range(2):
            mid[omega, (2 * group + part) * NB : (2 * group + part + 1) * NB, :] = jnp.where(
                tall < count,
                out[part * NB : (part + 1) * NB],
                shifted(out[(2 + part) * NB : (3 + part) * NB], count),
            )

    def beta_sum(step, carry):
        if with_rest:
            rows = pl.ds(pl.multiple_of(step * NB, NB), NB)
            first, second, turn = ga[rows, :], gc[rows, :], 3
        else:
            first = ga[pl.ds(pl.multiple_of(step * 2 * NB, NB), NB), :]
            second, turn = ga[pl.ds(pl.multiple_of(step * 2 * NB + NB, NB), NB), :], 2
        data = jnp.concatenate(
            [
                jnp.concatenate([first, second], 1),
                jnp.concatenate([shifted(first, 2), shifted(second, turn)], 1),
            ],
            0,
        )
        out = dot3((high_ref[...], low_ref[...]), split(data))
        if with_rest:
            store(step, 0, out[:, :LANES], 2)
            store(step, 1, out[:, LANES:], 1)
        else:
            store(2 * step, 0, out[:, :LANES], 2)
            store(2 * step + 1, 0, out[:, LANES:], 2)
        return carry

    lax.fori_loop(0, NW if with_rest else NW // 2, beta_sum, 0)

    which = lane_group((8, LANES))
    half_w = NW // 2

    def omega_sum(step, carry):
        row = pl.multiple_of(step * 8, 8)
        rows = pl.ds(row, 8)
        for group in range(2 if with_rest else 1):
            re = [mid[w, pl.ds(row + 2 * group * NB, 8), :] for w in range(NW)]
            im = [mid[w, pl.ds(row + (2 * group + 1) * NB, 8), :] for w in range(NW)]
            cos_terms = [re[0]] + [re[w] + re[NW - w] for w in range(1, half_w)] + [re[half_w]]
            sin_terms = [None] + [im[w] - im[NW - w] for w in range(1, half_w)]
            even = cosine_sums(cos_terms)
            odd = sine_sums(sin_terms)
            out = [None] * NW
            out[0] = even[0]
            out[half_w] = even[half_w]
            for t in range(1, half_w):
                out[t] = even[t] - odd[t]
                out[NW - t] = even[t] + odd[t]
            if group == 0:
                for t in range(half_w):
                    field_ref[t, rows, :] = halves(out[t], out[t + half_w], which < 2)
                    span_ref[t, rows, :] = jnp.where(which < 2, shifted(out[t], 2), out[t + half_w])
            else:
                for t in range(8):
                    for target, start in ((field_ref, 0), (span_ref, 1)):
                        target[half_w + t, rows, :] = join(
                            [shifted(out[t + 8 * k], k - start) for k in range(4)], which
                        )
        return carry

    lax.fori_loop(0, NB // 8, omega_sum, 0)


def force_kernel(
    with_rest, pos_ref, flow_ref, field_ref, other_ref, span_ref, mean_ref, wall_ref, high_ref, low_ref,
    out_ref, force, mid, na, nc, rest_rows,
):
    sources = out_ref.shape[0]
    full = M // sources
    half = full // 2
    wall = split(wall_ref[...])
    half_w = NW // 2
    tall = lane_group((NB, LANES))
    is_even = (tall % 2) == 0

    def products(step, carry):
        def one(row, v, w):
            both = jnp.concatenate([field_ref[row], other_ref[row]], 1)
            force[row] = -(v * dot3(split(both), wall) + w * span_ref[row])

        pair = [flow_ref[step], flow_ref[step + 8]]
        for k in range(2):
            one(
                step + 8 * k,
                jnp.where(is_even, pair[k], shifted(pair[k], 1)),
                jnp.where(is_even, shifted(pair[k], 3), pair[k]),
            )
        if with_rest:
            one(
                step + half_w,
                jnp.where(is_even, pair[0], shifted(pair[1], 1)),
                jnp.where(is_even, shifted(pair[0], 3), pair[1]),
            )
        return carry

    lax.fori_loop(0, 8, products, 0)

    def time_sum(step, carry):
        row = pl.multiple_of(step * 8, 8)
        rows = pl.ds(row, 8)
        for group in range(2 if with_rest else 1):
            if group == 0:
                packed = [force[t, rows, :] for t in range(half_w)]
                values = packed + [shifted(value, 2) for value in packed]
            else:
                packed = [force[half_w + t, rows, :] for t in range(8)]
                values = [shifted(packed[t % 8], -(t // 8)) for t in range(NW)]
            cos_terms = (
                [values[0]]
                + [values[t] + values[NW - t] for t in range(1, half_w)]
                + [values[half_w]]
            )
            sin_terms = [None] + [values[NW - t] - values[t] for t in range(1, half_w)]
            even = cosine_sums(cos_terms)
            odd = sine_sums(sin_terms)
            lanes = slice(group * LANES, (group + 1) * LANES)
            zero = jnp.zeros((8, LANES), F32)
            for w in range(half_w + 1):
                mid[w, rows, lanes] = even[w]
                mid[w, pl.ds(row + NB, 8), lanes] = odd[w] if 0 < w < half_w else zero
        return carry

    lax.fori_loop(0, NB // 8, time_sum, 0)

    def span_sum(omega, carry):
        out = dot3((high_ref[...], low_ref[...]), split(mid[omega]))
        rows = pl.ds(pl.multiple_of(omega * NB, NB), NB)
        na[rows, :] = halves(out[:NB, :LANES], out[NB:, :LANES], tall < 2)
        if with_rest:
            nc[rows, :] = jnp.where(tall < 1, out[:NB, LANES:], shifted(out[NB:, LANES:], 1))
        return carry

    lax.fori_loop(0, half_w + 1, span_sum, 0)

    def collect(source, carry):
        def rows_of(step, inner):
            row = pl.multiple_of(step * 8, 8)
            for side in range(2):
                first = row + side * half
                for u in range(8):
                    where = pos_ref[source * full + first + u]
                    out_ref[source, pl.ds(first + u, 1), :] = na[pl.ds(where, 1), :]
                    if with_rest:
                        rest_rows[side, pl.ds(row + u, 1), :] = nc[pl.ds(where, 1), :]
            return inner

        lax.fori_loop(0, half // 8, rows_of, 0)
        if with_rest:
            out_ref[source, full : full + half, :] = halves(
                rest_rows[0], rest_rows[1], lane_group((half, LANES)) < 2
            )
        else:
            out_ref[source, full : full + 8, :] = mean_ref[...]
        return carry

    lax.fori_loop(0, sources, collect, 0)


def sweep_kernel(
    amp_ref, first_ref, second_ref, base_ref, matrix_ref, inverse_ref, rim_ref, wave_ref, freq_ref, sign_ref,
    out_ref, right, current, residual, flow,
):
    half = amp_ref.shape[0] // 80
    full = 2 * half
    rows_in = 16
    which = lane_group((rows_in, LANES))
    which8 = lane_group((8, LANES))
    for tile in range(4):
        mean = join([shifted(first_ref[4 * tile + k, full : full + 8, :], k - 1) for k in range(4)], which8)
        flow[:, tile * LANES : (tile + 1) * LANES] = mean + base_ref[:, tile * LANES : (tile + 1) * LANES]
    inverse = [split(inverse_ref[g]) for g in range(2)]

    def chunk(step, carry):
        row = pl.multiple_of(step * rows_in, rows_in)
        for tile in range(4):
            lanes = slice(tile * LANES, (tile + 1) * LANES)
            rest = [second_ref[4 * tile + k, pl.ds(row + full, rows_in), :] for k in range(4)]
            for side in range(2):
                rows = pl.ds(row + side * half, rows_in)
                sign = sign_ref[rows, :]
                got = [
                    [ref[4 * tile + k, rows, :] for k in range(4)] for ref in (second_ref, first_ref)
                ]
                for part in range(2):
                    for c in range(5):
                        if c < 4:
                            source, place = got[c // 2], 2 * part + c % 2
                        else:
                            source, place = rest, 2 * side + part
                        value = join([shifted(source[k], k - place) for k in range(4)], which)
                        if part == 1:
                            value = value * sign
                        own = channel(amp_ref, 5 * part + c, row + side * half, rows_in, tile)
                        place = slice((5 * part + c) * 32 + side * 16, (5 * part + c) * 32 + side * 16 + 16)
                        current[place, lanes] = own
                        right[place, lanes] = own + march_step * value

        for sweep in range(SWEEPS):
            high, low = split(current[...])
            residual[...] = right[...] + coupling * (dot(high, rim_ref[...]) + dot(low, rim_ref[...]))
            for tile in range(4):
                lanes = slice(tile * LANES, (tile + 1) * LANES)
                for side in range(2):
                    rows = pl.ds(row + side * half, rows_in)
                    rotation = phase_gain * wave_ref[rows, :] * flow[0:1, lanes] - freq_ref[rows, :]
                    x = [current[c * 32 + side * 16 : c * 32 + side * 16 + 16, lanes] for c in range(10)]
                    for part in range(2):
                        for c in range(5):
                            total = rotation * x[5 * (1 - part) + c]
                            if part == 0:
                                total = -total
                            for j in range(5):
                                total = total + matrix_ref[5 * c + j : 5 * c + j + 1, lanes] * x[5 * part + j]
                            place = slice((5 * part + c) * 32 + side * 16, (5 * part + c) * 32 + side * 16 + 16)
                            residual[place, lanes] = residual[place, lanes] - total
            for g in range(2):
                lanes = slice(g * 256, (g + 1) * 256)
                current[:, lanes] = dot3(split(residual[:, lanes]), inverse[g])
        for c in range(10):
            for side in range(2):
                for tile in range(4):
                    offset = (row + side * half) * 40 + (c % 5) * 8 + tile * 2 + c // 5
                    out_ref[pl.ds(offset, rows_in, stride=40), :] = current[
                        c * 32 + side * 16 : c * 32 + side * 16 + 16, tile * LANES : (tile + 1) * LANES
                    ]
        return carry

    lax.fori_loop(0, half // rows_in, chunk, 0)


def local_fast(amplitudes, mode_table, slab_map, base_flow, base_coupling, slab_inverse, wall_operator):
    local_modes = amplitudes.shape[0]
    points = amplitudes.shape[3]
    groups = lax.axis_size("modes")
    me = lax.axis_index("modes")
    half = local_modes // 2
    vmem = pl.BlockSpec(memory_space=pltpu.VMEM)
    smem = pl.BlockSpec(memory_space=pltpu.SMEM)
    params = pltpu.CompilerParams(vmem_limit_bytes=VMEM_BYTES)
    width = slab_inverse.shape[1]

    def cost(micros):
        return pl.CostEstimate(flops=micros * 10**9, bytes_accessed=micros * 3 * 10**6, transcendentals=0)


    omega_index = mode_table[:, 0]
    beta_index = mode_table[:, 1]
    grid_pos = omega_index * NB + beta_index
    mirrored = omega_index > NW // 2
    back_pos = jnp.where(mirrored, (NW - omega_index) * NB + (NB - beta_index) % NB, grid_pos)
    local_table = lax.dynamic_slice_in_dim(mode_table, me * local_modes, local_modes)
    omega_local = local_table[:, 0:1]
    beta_local = local_table[:, 1:2]
    signed = jnp.where(beta_local >= NB // 2, beta_local - NB, beta_local)
    wave_local = 2.0 * signed.astype(F32) / NB
    freq_local = omega_step * omega_local.astype(F32)
    sign_local = jnp.where(omega_local > NW // 2, -1.0, 1.0).astype(F32)

    part = lax.rem(me, 2) * SHARE
    rows = lax.dynamic_slice_in_dim(wall_operator, part, SHARE, 0)
    mine = lax.dynamic_slice_in_dim(rows, part, SHARE, 1)
    theirs = lax.dynamic_slice_in_dim(rows, SHARE - part, SHARE, 1)
    eye = jnp.eye(4, dtype=F32)

    def blocks(value):
        size = value.shape[0]
        return (eye[:, None, :, None] * value.T[None, :, None, :]).reshape(4 * size, 4 * size)

    wall = jnp.concatenate([blocks(mine), blocks(theirs)], 0)
    turned = jnp.swapaxes(slab_inverse, 1, 2).reshape(2, 4, width, 1, width)
    inverse = (turned * eye[None, :, None, :, None]).reshape(2, 4 * width, 4 * width)
    source, weight = interface_table(slab_map, slab_inverse.shape[0], width)
    rim = ((jnp.arange(points, dtype=jnp.int32)[:, None] == source[None, :]) & (weight[None, :] > 0)).astype(BF16)

    tiled = amplitudes.reshape(local_modes, 2, 5, points // LANES, LANES)
    amp = jnp.transpose(tiled, (0, 2, 3, 1, 4)).reshape(local_modes * 40, LANES)
    synthesis = [jnp.asarray(part) for part in split_np(synthesis_matrix())]
    analysis = [jnp.asarray(part) for part in split_np(analysis_matrix())]
    half_w = NW // 2
    rows_back = (half_w + 1) * NB

    def pack(kernel, source, rows, name):
        return pl.pallas_call(
            kernel,
            out_shape=jax.ShapeDtypeStruct((groups, rows, LANES), F32),
            in_specs=[vmem],
            out_specs=vmem,
            compiler_params=params,
            cost_estimate=cost(6),
            name=name,
        )(source)

    def exchange(message):
        return lax.all_to_all(message, "modes", split_axis=0, concat_axis=0, tiled=True)

    def physical(arrived, with_rest):
        count = half_w + (8 if with_rest else 0)
        block = jax.ShapeDtypeStruct((count, NB, LANES), F32)
        kinds = 2 if with_rest else 1
        return pl.pallas_call(
            functools.partial(physical_kernel, with_rest),
            out_shape=[block, block, jax.ShapeDtypeStruct((8, LANES), F32)],
            in_specs=[smem, vmem, vmem, vmem],
            out_specs=[vmem, vmem, vmem],
            scratch_shapes=[
                pltpu.VMEM((M, LANES), F32),
                pltpu.VMEM((M if with_rest else 8, LANES), F32),
                pltpu.VMEM((NW, 2 * kinds * NB, LANES), F32),
            ],
            compiler_params=params,
            cost_estimate=cost(15 * kinds),
            name="physical" + str(kinds),
        )(grid_pos, arrived, *synthesis)

    def swap(field):
        return lax.ppermute(field, "modes", [(i, i ^ 1) for i in range(groups)])

    def forces(flow, field, other, span, mean, with_rest):
        kinds = 2 if with_rest else 1
        return pl.pallas_call(
            functools.partial(force_kernel, with_rest),
            out_shape=jax.ShapeDtypeStruct((groups, 3 * half if with_rest else 2 * half + 8, LANES), F32),
            in_specs=[smem] + [vmem] * 8,
            out_specs=vmem,
            scratch_shapes=[
                pltpu.VMEM((half_w + 8, NB, LANES), F32),
                pltpu.VMEM((half_w + 1, 2 * NB, kinds * LANES), F32),
                pltpu.VMEM((rows_back, LANES), F32),
                pltpu.VMEM((rows_back if with_rest else 8, LANES), F32),
                pltpu.VMEM((2, half, LANES), F32),
            ],
            compiler_params=params,
            cost_estimate=cost(10 * kinds),
            name="force" + str(kinds),
        )(back_pos, flow, field, other, span, mean, wall, *analysis)

    first_message = pack(pack_first_kernel, amp, 2 * half, "pack1")
    first_message, later = lax.optimization_barrier((first_message, amp))
    first = exchange(first_message)
    second_message = pack(pack_second_kernel, later, 3 * half, "pack2")
    second = exchange(second_message)
    first, second_message = lax.optimization_barrier((first, second_message))
    flow, flow_span, mean = physical(first, False)
    first_force = forces(flow, flow, swap(flow), flow_span, mean, False)
    first_force, second = lax.optimization_barrier((first_force, second))
    first_back = exchange(first_force)
    field, span, unused = physical(second, True)
    second_back = exchange(forces(flow, field, swap(field), span, unused, True))

    marched = pl.pallas_call(
        sweep_kernel,
        out_shape=jax.ShapeDtypeStruct((local_modes * 40, LANES), F32),
        in_specs=[vmem] * 10,
        out_specs=vmem,
        scratch_shapes=[pltpu.VMEM((320, points), F32)] * 3 + [pltpu.VMEM((8, points), F32)],
        compiler_params=params,
        name="sweeps",
    )(amp, first_back, second_back, base_flow[None, :], base_coupling, inverse, rim, wave_local, freq_local, sign_local)
    ordered = marched.reshape(local_modes, 5, points // LANES, 2, LANES)
    return jnp.transpose(ordered, (0, 3, 1, 2, 4)).reshape(local_modes, 2, 5, points)


def run(amplitudes, mode_table, slab_map, base_flow, base_coupling, slab_inverse, wall_operator):
    groups = lax.axis_size("modes")
    fits = (
        amplitudes.shape == (256, 2, 5, 512)
        and groups * SHARE == amplitudes.shape[3]
        and slab_inverse.shape == (8, 2 * SHARE, 2 * SHARE)
    )
    chosen = local_fast if fits else local
    return chosen(
        amplitudes, mode_table, slab_map, base_flow, base_coupling, slab_inverse, wall_operator
    )


def solution(mesh):
    return jax.shard_map(
        run,
        mesh=mesh,
        in_specs=(
            P(("runs", "modes"), None, None, None),
            P(),
            P(),
            P("runs"),
            P("runs", None),
            P(),
            P(),
        ),
        out_specs=P(("runs", "modes"), None, None, None),
        check_vma=False,
    )
```
